32 devices in a mesh: groups: 2 (over y), seq: 4 (over z), head: 2 (over x), rep: 2 (over core).
Axes of the slice: x: 2, y: 2, z: 4, core: 2. Of those that a mesh axis runs over, the one named last changes fastest.
Arguments:
- queries: bfloat16 [8192, 8, 128], P(('groups', 'seq', 'rep'), 'head'), parts along dimension 0, may hold values from -1.796875 to 1.796875
- keys: bfloat16 [8192, 8, 128], P(('groups', 'seq', 'rep'), 'head'), parts along dimension 0, may hold values from -1.796875 to 1.796875
- values: bfloat16 [8192, 8, 128], P(('groups', 'seq', 'rep'), 'head'), parts along dimension 0, may hold values from -6 to 6
- out_grad: bfloat16 [8192, 8, 128], P(('groups', 'seq', 'rep'), 'head'), parts along dimension 0, may hold values from -1.796875 to 1.796875
- level_table: float32 [7, 8], P(None, 'head'), may hold values from 0.25 to 2
Outputs:
- attended: bfloat16 [8192, 8, 128], P(('groups', 'seq', 'rep'), 'head'), parts along dimension 0
- query_grad: bfloat16 [8192, 8, 128], P(('groups', 'seq', 'rep'), 'head'), parts along dimension 0
- key_grad: bfloat16 [8192, 8, 128], P(('groups', 'seq', 'rep'), 'head'), parts along dimension 0
- value_grad: bfloat16 [8192, 8, 128], P(('groups', 'seq', 'rep'), 'head'), parts along dimension 0
The draws below stay inside these ranges and needn't reach their ends.
There are 2 independent parts, one for each index of `groups`. The reference program is written for one: setup_inputs(seed, part) draws one part's arguments, and reference() takes and returns one part's arrays. A program takes and returns all parts, laid end to end along the dimension named above; an argument that names none is the same for every part. Nothing has to cross between parts.
All inputs are finite; a program needn't handle non-finite values.
Results may differ from the reference program's by a relative error of at most 0.001.
Values sent between devices are 32-bit elements; how exact they have to be, the bound alone decides.
No kernel may reach another device: no remote copies, remote signals or barrier semaphores. Data moves between devices by JAX's collectives and lax.ppermute only.
A program may use at most 64 MiB of HBM per device.

```python
import math
import jax
import jax.numpy as jnp
from jax import lax

D = 128
HEADS = 8
BLOCK = 64
TOKENS = 4096
LEVELS = 7


def steps_of(rng, dims, shards, least, high):
    loudness = 1.0
    for dim, parts in shards:
        draws = jax.random.uniform(jax.random.fold_in(jax.random.fold_in(rng, 6), dim), (parts,), jnp.float32, least / len(shards), high / len(shards))
        loudness = loudness * jnp.repeat(jnp.exp(draws), dims[dim] // parts).reshape((-1,) + (1,) * (len(dims) - 1 - dim))
    return loudness


def normal_values(stream_key, dims, spread, limit, shards=(), held_as=jnp.bfloat16):
    values = spread * jax.random.normal(stream_key, dims, jnp.float32)
    if shards:
        values = values * steps_of(stream_key, dims, shards, -0.22, 0.18)
    return jnp.clip(values, -limit, limit).astype(held_as)


def setup_inputs(seed: int = 0, part: int = 0) -> dict:
    key_of = jax.random.split(jax.random.key(seed), 6)
    part_keys = jax.random.split(jax.random.fold_in(key_of[5], part), 6)
    return {
        "queries": normal_values(part_keys[0], (TOKENS, HEADS, D), 0.3, 1.796875, ((0, 8), (1, 2))),
        "keys": normal_values(part_keys[1], (TOKENS, HEADS, D), 0.3, 1.796875, ((0, 8), (1, 2))),
        "values": normal_values(part_keys[2], (TOKENS, HEADS, D), 1.0, 6.0, ((0, 8), (1, 2))),
        "out_grad": normal_values(part_keys[3], (TOKENS, HEADS, D), 0.3, 1.796875, ((0, 8), (1, 2))),
        "level_table": jnp.clip(jnp.exp(math.log(2.0) - 2.0794415 * jax.random.uniform(key_of[4], (LEVELS, HEADS), jnp.float32) ** steps_of(key_of[4], (LEVELS, HEADS), ((1, 2),), -0.2, 0.2)), 0.25, 2.0),
    }


def product(form, left, right):
    return jnp.einsum(form, left, right, precision=lax.Precision.HIGHEST)

def bit_length(numbers, top):
    total = jnp.zeros(numbers.shape, jnp.int32)
    for shift in range(top):
        total = total + (jnp.right_shift(numbers, shift) > 0).astype(jnp.int32)
    return total

def scaled_weights(level_table):
    count = level_table.shape[0]
    power = jnp.maximum(jnp.arange(count, dtype=jnp.int32) - 1, 0).astype(jnp.float32)
    scale = 1.0 / jnp.sqrt(jnp.float32(BLOCK) * jnp.exp2(power))
    return level_table * scale[:, None]

def head_pass(packed):
    queries, keys, values, out_grad, column = packed
    count = TOKENS // BLOCK
    shape3 = (count, BLOCK, queries.shape[-1])
    qb = queries.astype(jnp.float32).reshape(shape3)
    kb = keys.astype(jnp.float32).reshape(shape3)
    vb = values.astype(jnp.float32).reshape(shape3)
    gb = out_grad.astype(jnp.float32).reshape(shape3)
    order = jnp.arange(BLOCK, dtype=jnp.int32)
    causal = (order[:, None] >= order[None, :]).astype(jnp.float32) * column[0]
    scores = product('ncd,nsd->ncs', qb, kb) * causal
    grads = product('ncd,nsd->ncs', gb, vb) * causal
    key_state = product('ncd,nce->nde', kb, vb)
    query_state = product('ncd,nce->nde', qb, gb)
    blocks = jnp.arange(count, dtype=jnp.int32)
    level = bit_length(jnp.bitwise_xor(blocks[:, None], blocks[None, :]), LEVELS)
    onehot = (level[:, :, None] == jnp.arange(LEVELS, dtype=jnp.int32)).astype(jnp.float32)
    earlier = (blocks[None, :] < blocks[:, None]).astype(jnp.float32)
    coef = product('nml,l->nm', onehot, column) * earlier
    read_state = product('nm,mde->nde', coef, key_state)
    back_state = product('nm,nde->mde', coef, query_state)
    attended = product('ncs,nse->nce', scores, vb) + product('ncd,nde->nce', qb, read_state)
    query_grad = product('ncs,nsd->ncd', grads, kb) + product('nce,nde->ncd', gb, read_state)
    key_grad = product('ncs,ncd->nsd', grads, qb) + product('nce,nde->ncd', vb, back_state)
    value_grad = product('ncs,nce->nse', scores, gb) + product('ncd,nde->nce', kb, back_state)
    flat = (TOKENS, queries.shape[-1])
    return (attended.reshape(flat), query_grad.reshape(flat), key_grad.reshape(flat), value_grad.reshape(flat))

def reference(queries, keys, values, out_grad, level_table):
    weights = scaled_weights(level_table)
    packed = (jnp.transpose(queries, (1, 0, 2)), jnp.transpose(keys, (1, 0, 2)), jnp.transpose(values, (1, 0, 2)), jnp.transpose(out_grad, (1, 0, 2)), jnp.transpose(weights, (1, 0)))
    results = lax.map(head_pass, packed)
    attended = jnp.transpose(results[0], (1, 0, 2)).astype(jnp.bfloat16)
    query_grad = jnp.transpose(results[1], (1, 0, 2)).astype(jnp.bfloat16)
    key_grad = jnp.transpose(results[2], (1, 0, 2)).astype(jnp.bfloat16)
    value_grad = jnp.transpose(results[3], (1, 0, 2)).astype(jnp.bfloat16)
    return (attended, query_grad, key_grad, value_grad)
```

```python
import functools
import math

import jax
import jax.numpy as jnp
import numpy as np
from jax import lax
from jax.experimental import pallas as pl
from jax.experimental.pallas import tpu as pltpu
from jax.sharding import PartitionSpec as P

BLOCK = 64
TILE = 256
F32 = jnp.float32
BF16 = jnp.bfloat16


def swap_cores(block):
    return lax.ppermute(block, "rep", [(0, 1), (1, 0)])


def swap_chips(block, mask):
    count = lax.axis_size("seq")
    return lax.ppermute(block, "seq", [(chip, chip ^ mask) for chip in range(count)])


def level_scale(level):
    return float(np.float32(1.0) / np.sqrt(np.float32(BLOCK * 2 ** max(level - 1, 0))))


def dot_tn(left, right):
    return lax.dot_general(left, right, (((0,), (0,)), ((), ())), preferred_element_type=F32)


def dot_nt(left, right):
    return lax.dot_general(left, right, (((1,), (1,)), ((), ())), preferred_element_type=F32)


def dot_nn(left, right):
    return lax.dot_general(left, right, (((1,), (0,)), ((), ())), preferred_element_type=F32)


def split(value):
    high = value.astype(BF16)
    return high, (value - high.astype(F32)).astype(BF16)


def state_kernel(heads, q_ref, k_ref, v_ref, g_ref, send_ref, keep_ref, per_head_ref, wide):
    rows = q_ref.shape[0] // heads
    half = heads // 2
    core = lax.axis_index("rep")
    for which, ref in enumerate((q_ref, k_ref, v_ref, g_ref)):
        wide[which] = ref[...].astype(F32)
    for which in range(4):
        for head in range(heads):
            per_head_ref[which, head] = wide[which, pl.ds(head, rows, stride=heads), :].astype(BF16)
    for place in range(half):
        for owner, out_ref in ((1 - core, send_ref), (core, keep_ref)):
            head = owner * half + place
            out_ref[0, place] = dot_tn(per_head_ref[1, head], per_head_ref[2, head])
            out_ref[1, place] = dot_tn(per_head_ref[0, head], per_head_ref[3, head])


def states(queries, keys, values, out_grad):
    rows, heads, width = queries.shape
    flat = [array.reshape(rows * heads, width) for array in (queries, keys, values, out_grad)]
    half = (2, heads // 2, width, width)
    return pl.pallas_call(
        functools.partial(state_kernel, heads),
        out_shape=(
            jax.ShapeDtypeStruct(half, F32),
            jax.ShapeDtypeStruct(half, F32),
            jax.ShapeDtypeStruct((4, heads, rows, width), BF16),
        ),
        in_specs=[pl.BlockSpec(memory_space=pltpu.VMEM)] * 4,
        out_specs=[pl.BlockSpec(memory_space=pltpu.VMEM)] * 3,
        scratch_shapes=[pltpu.VMEM((4, rows * heads, width), F32)],
        compiler_params=pltpu.CompilerParams(vmem_limit_bytes=24 * 2**20),
        name="states",
    )(*flat)


def local_kernel(table_ref, per_head_ref, out_ref):
    head = pl.program_id(0)
    rows = per_head_ref.shape[1]
    tiles = rows // TILE
    weight = [table_ref[level, head] * level_scale(level) for level in range((rows // BLOCK).bit_length())]
    row = lax.broadcasted_iota(jnp.int32, (TILE, TILE), 0)
    column = lax.broadcasted_iota(jnp.int32, (TILE, TILE), 1)
    apart = jnp.bitwise_xor(row // BLOCK, column // BLOCK)
    mask = jnp.where(apart == 0, weight[0], weight[1])
    for level in range(2, (TILE // BLOCK).bit_length()):
        mask = jnp.where(apart >= 1 << (level - 1), weight[level], mask)
    mask = jnp.where(row >= column, mask, 0.0)
    part = [[per_head_ref[which, pl.ds(tile * TILE, TILE), :] for tile in range(tiles)] for which in range(4)]
    queries, keys, values, out_grad = part
    results = [[None] * tiles for _ in range(4)]

    def add(which, tile, value):
        held = results[which][tile]
        results[which][tile] = value if held is None else held + value

    for later in range(tiles):
        for earlier in range(later + 1):
            scale = mask if later == earlier else weight[(TILE // BLOCK).bit_length() - 1 + (later ^ earlier).bit_length()]
            scores = split(dot_nt(queries[later], keys[earlier]) * scale)
            grads = split(dot_nt(out_grad[later], values[earlier]) * scale)
            for piece in scores:
                add(0, later, dot_nn(piece, values[earlier]))
                add(3, earlier, dot_tn(piece, out_grad[later]))
            for piece in grads:
                add(1, later, dot_nn(piece, keys[earlier]))
                add(2, earlier, dot_tn(piece, queries[later]))
    for which in range(4):
        for tile in range(tiles):
            out_ref[which, pl.ds(tile * TILE, TILE), :] = results[which][tile]


def local_part(level_table, per_head):
    _, heads, rows, width = per_head.shape
    return pl.pallas_call(
        local_kernel,
        grid=(heads,),
        out_shape=jax.ShapeDtypeStruct((4, heads, rows, width), F32),
        in_specs=[
            pl.BlockSpec(memory_space=pltpu.SMEM),
            pl.BlockSpec((4, None, rows, width), lambda head: (0, head, 0, 0)),
        ],
        out_specs=pl.BlockSpec((4, None, rows, width), lambda head: (0, head, 0, 0)),
        compiler_params=pltpu.CompilerParams(vmem_limit_bytes=24 * 2**20),
        cost_estimate=pl.CostEstimate(flops=3 * 10**9, bytes_accessed=6 * 2**20, transcendentals=0),
        name="local",
    )(level_table, per_head)


def final_kernel(per_head_ref, local_ref, far_ref, *refs):
    out_refs, wide = refs[:4], refs[4]
    heads, rows = per_head_ref.shape[1:3]
    for head in range(heads):
        keys_far = split(far_ref[0, head])
        queries_far = split(far_ref[1, head])
        q, k, v, g = (per_head_ref[which, head] for which in range(4))
        results = [local_ref[which, head] for which in range(4)]
        for piece in keys_far:
            results[0] += dot_nn(q, piece)
            results[1] += dot_nt(g, piece)
        for piece in queries_far:
            results[2] += dot_nt(v, piece)
            results[3] += dot_nn(k, piece)
        for which in range(4):
            wide[which, pl.ds(head, rows, stride=heads), :] = results[which]
    for which in range(4):
        out_refs[which][...] = wide[which].astype(BF16)


def final_part(per_head, local, far):
    _, heads, rows, width = per_head.shape
    outs = pl.pallas_call(
        final_kernel,
        out_shape=[jax.ShapeDtypeStruct((rows * heads, width), BF16)] * 4,
        in_specs=[pl.BlockSpec(memory_space=pltpu.VMEM)] * 3,
        out_specs=[pl.BlockSpec(memory_space=pltpu.VMEM)] * 4,
        scratch_shapes=[pltpu.VMEM((4, rows * heads, width), F32)],
        compiler_params=pltpu.CompilerParams(vmem_limit_bytes=24 * 2**20),
        name="final",
    )(per_head, local, far)
    return tuple(out.reshape(rows, heads, width) for out in outs)


def per_device(queries, keys, values, out_grad, level_table):
    rows, heads, width = queries.shape
    half = heads // 2
    chips = lax.axis_size("seq")
    core = lax.axis_index("rep")
    chip = lax.axis_index("seq")
    local_levels = (rows // BLOCK).bit_length()
    scale = jnp.array([level_scale(level) for level in range(level_table.shape[0])], F32)
    weights = level_table * scale[:, None]

    send, keep, per_head = states(queries, keys, values, out_grad)
    received = swap_cores(send)
    total = keep + received
    mine = []
    for mask in range(chips - 1, 0, -1):
        later = (chip ^ mask) < chip
        mine.append((mask, later, swap_chips(jnp.where(later, total[1], total[0]), mask)))
    near_other = swap_cores(jnp.where(core == 0, keep[0], keep[1]))
    near_mine = jnp.where(core == 0, received[1], received[0])
    local = local_part(level_table, per_head)

    own = lax.dynamic_slice_in_dim(weights, core * half, half, 1)[:, :, None, None]
    others = lax.dynamic_slice_in_dim(weights, (1 - core) * half, half, 1)[:, :, None, None]
    upper = (core == 1).astype(F32)
    far = []
    for table, near, pieces in (
        (own, near_mine, [piece for _, _, piece in mine]),
        (others, near_other, [swap_cores(piece) for _, _, piece in mine]),
    ):
        keys_far = upper * table[local_levels] * near
        queries_far = (1.0 - upper) * table[local_levels] * near
        for (mask, later, _), piece in zip(mine, pieces):
            term = table[local_levels + mask.bit_length()] * piece
            keys_far += jnp.where(later, term, 0.0)
            queries_far += jnp.where(later, 0.0, term)
        far.append(jnp.stack([keys_far, queries_far]))
    first = jnp.where(core == 0, far[0], far[1])
    second = jnp.where(core == 0, far[1], far[0])
    return final_part(per_head, local, jnp.concatenate([first, second], axis=1))


def solution(mesh):
    part = P(("groups", "seq", "rep"), "head", None)
    return jax.shard_map(
        per_device,
        mesh=mesh,
        in_specs=(part, part, part, part, P(None, "head")),
        out_specs=(part, part, part, part),
        check_vma=False,
    )
```

```python
import functools
import math

import jax
import jax.numpy as jnp
import numpy as np
from jax import lax
from jax.experimental import pallas as pl
from jax.experimental.pallas import tpu as pltpu
from jax.sharding import PartitionSpec as P

BLOCK = 64
TILE = 128
CHUNKS = 2
F32 = jnp.float32
BF16 = jnp.bfloat16


def swap_cores(block):
    return lax.ppermute(block, "rep", [(0, 1), (1, 0)])


def swap_chips(block, mask):
    count = lax.axis_size("seq")
    return lax.ppermute(block, "seq", [(chip, chip ^ mask) for chip in range(count)])


def level_scale(level):
    return float(np.float32(1.0) / np.sqrt(np.float32(BLOCK * 2 ** max(level - 1, 0))))


def dot_tn(left, right):
    return lax.dot_general(left, right, (((0,), (0,)), ((), ())), preferred_element_type=F32)


def dot_nt(left, right):
    return lax.dot_general(left, right, (((1,), (1,)), ((), ())), preferred_element_type=F32)


def dot_nn(left, right):
    return lax.dot_general(left, right, (((1,), (0,)), ((), ())), preferred_element_type=F32)


def split(value):
    high = value.astype(BF16)
    return high, (value - high.astype(F32)).astype(BF16)


def state_kernel(heads, q_ref, k_ref, v_ref, g_ref, send_ref, keep_ref, per_head_ref, narrow, wide, arrived):
    rows = q_ref.shape[0] // heads
    half = heads // 2
    core = lax.axis_index("rep")
    sources = (q_ref, k_ref, v_ref, g_ref)
    length = rows * heads // CHUNKS

    def fetch(which, chunk):
        span = pl.ds(chunk * length, length)
        return pltpu.make_async_copy(sources[which].at[span], narrow.at[which, span], arrived.at[which, chunk])

    pairs = ((1, 2), (0, 3))
    for pair in pairs:
        for which in pair:
            for chunk in range(CHUNKS):
                fetch(which, chunk).start()
    for kind, pair in enumerate(pairs):
        for which in pair:
            for chunk in range(CHUNKS):
                fetch(which, chunk).wait()
            wide[which] = narrow[which].astype(F32)
            for head in range(heads):
                per_head_ref[which, head] = wide[which, pl.ds(head, rows, stride=heads), :].astype(BF16)
        for place in range(half):
            for owner, out_ref in ((1 - core, send_ref), (core, keep_ref)):
                head = owner * half + place
                out_ref[kind, place] = dot_tn(per_head_ref[pair[0], head], per_head_ref[pair[1], head])


def states(heads, flat):
    rows, width = flat[0].shape[0] // heads, flat[0].shape[1]
    half = (2, heads // 2, width, width)
    return pl.pallas_call(
        functools.partial(state_kernel, heads),
        out_shape=(
            jax.ShapeDtypeStruct(half, F32),
            jax.ShapeDtypeStruct(half, F32),
            jax.ShapeDtypeStruct((4, heads, rows, width), BF16),
        ),
        in_specs=[pl.BlockSpec(memory_space=pltpu.HBM)] * 4,
        out_specs=[pl.BlockSpec(memory_space=pltpu.VMEM)] * 3,
        scratch_shapes=[
            pltpu.VMEM((4, rows * heads, width), BF16),
            pltpu.VMEM((4, rows * heads, width), F32),
            pltpu.SemaphoreType.DMA((4, CHUNKS)),
        ],
        compiler_params=pltpu.CompilerParams(vmem_limit_bytes=24 * 2**20),
        name="states",
    )(*[pltpu.with_memory_space_constraint(array, pltpu.HBM) for array in flat])


def local_kernel(table_ref, per_head_ref, out_ref):
    head = pl.program_id(0)
    rows = per_head_ref.shape[1]
    tiles = rows // TILE
    inner = (TILE // BLOCK).bit_length()
    weight = [table_ref[level, head] * level_scale(level) for level in range(inner + tiles.bit_length() - 1)]
    row = lax.broadcasted_iota(jnp.int32, (TILE, TILE), 0)
    column = lax.broadcasted_iota(jnp.int32, (TILE, TILE), 1)
    apart = jnp.bitwise_xor(row // BLOCK, column // BLOCK)
    level_mask = jnp.where(apart == 0, weight[0], weight[1])
    for level in range(2, inner):
        level_mask = jnp.where(apart >= 1 << (level - 1), weight[level], level_mask)
    lower = jnp.where(row >= column, level_mask, 0.0)
    upper = jnp.where(row <= column, level_mask, 0.0)
    part = [[per_head_ref[which, pl.ds(tile * TILE, TILE), :] for tile in range(tiles)] for which in range(4)]
    queries, keys, values, out_grad = part

    def sums(states):
        table = {(0, tile): states[tile] for tile in range(tiles)}
        for bit in range(1, tiles.bit_length() - 1):
            for group in range(tiles >> bit):
                table[bit, group] = table[bit - 1, 2 * group] + table[bit - 1, 2 * group + 1]
        return table

    def gather(table, tile, side):
        total = None
        for bit in range(tiles.bit_length() - 1):
            if (tile >> bit) % 2 == side:
                term = weight[inner + bit] * table[bit, (tile >> bit) ^ 1]
                total = term if total is None else total + term
        return [] if total is None else split(total)

    key_sums = sums([dot_tn(keys[tile], values[tile]) for tile in range(tiles)])
    query_sums = sums([dot_tn(queries[tile], out_grad[tile]) for tile in range(tiles)])
    for tile in range(tiles):
        q, k, v, g = (array[tile] for array in part)
        read, back = gather(key_sums, tile, 1), gather(query_sums, tile, 0)
        terms = (
            (dot_nt(q, k) * lower, v, q, read, dot_nn),
            (dot_nt(g, v) * lower, k, g, read, dot_nt),
            (dot_nt(v, g) * upper, q, v, back, dot_nt),
            (dot_nt(k, q) * upper, g, k, back, dot_nn),
        )
        for which, (inside, other, mine, pieces, multiply) in enumerate(terms):
            result = dot_nn(jnp.concatenate(split(inside), 1), jnp.concatenate([other, other], 0))
            for piece in pieces:
                result += multiply(mine, piece)
            out_ref[which, pl.ds(tile * TILE, TILE), :] = result


def local_part(level_table, per_head):
    _, heads, rows, width = per_head.shape
    block = pl.BlockSpec((4, None, rows, width), lambda head: (0, head, 0, 0))
    return pl.pallas_call(
        local_kernel,
        grid=(heads,),
        out_shape=jax.ShapeDtypeStruct((4, heads, rows, width), F32),
        in_specs=[pl.BlockSpec(memory_space=pltpu.SMEM), block],
        out_specs=block,
        compiler_params=pltpu.CompilerParams(vmem_limit_bytes=24 * 2**20),
        cost_estimate=pl.CostEstimate(flops=3 * 10**9, bytes_accessed=6 * 2**20, transcendentals=0),
        name="local",
    )(level_table, per_head)


def final_kernel(per_head_ref, local_ref, far_ref, *refs):
    out_refs, (wide, narrow, left) = refs[:4], refs[4:]
    heads, rows = per_head_ref.shape[1:3]
    far = [[split(far_ref[kind, head]) for head in range(heads)] for kind in range(2)]
    plan = ((0, 0, 0, dot_nn), (1, 3, 0, dot_nt), (2, 2, 1, dot_nt), (3, 1, 1, dot_nn))
    copies = []
    for which, source, kind, multiply in plan:
        for head in range(heads):
            result = local_ref[which, head]
            for piece in far[kind][head]:
                result += multiply(per_head_ref[source, head], piece)
            wide[which, pl.ds(head, rows, stride=heads), :] = result
        narrow[which] = wide[which].astype(BF16)
        copy = pltpu.make_async_copy(narrow.at[which], out_refs[which], left.at[which])
        copy.start()
        copies.append(copy)
    for copy in copies:
        copy.wait()


def final_part(per_head, local, far):
    _, heads, rows, width = per_head.shape
    outs = pl.pallas_call(
        final_kernel,
        out_shape=[jax.ShapeDtypeStruct((rows * heads, width), BF16)] * 4,
        in_specs=[pl.BlockSpec(memory_space=pltpu.VMEM)] * 3,
        out_specs=[pl.BlockSpec(memory_space=pltpu.HBM)] * 4,
        scratch_shapes=[
            pltpu.VMEM((4, rows * heads, width), F32),
            pltpu.VMEM((4, rows * heads, width), BF16),
            pltpu.SemaphoreType.DMA((4,)),
        ],
        compiler_params=pltpu.CompilerParams(vmem_limit_bytes=24 * 2**20),
        name="final",
    )(per_head, local, far)
    return tuple(out.reshape(rows, heads, width) for out in outs)


def per_device(queries, keys, values, out_grad, level_table):
    rows, heads, width = queries.shape
    half = heads // 2
    chips = lax.axis_size("seq")
    core = lax.axis_index("rep")
    chip = lax.axis_index("seq")
    local_levels = (rows // BLOCK).bit_length()
    scale = jnp.array([level_scale(level) for level in range(level_table.shape[0])], F32)
    weights = level_table * scale[:, None]

    flat = [array.reshape(rows * heads, width) for array in (queries, keys, values, out_grad)]
    send, keep, per_head = states(heads, flat)
    received = swap_cores(send)
    total = keep + received
    masks = range(chips - 1, 0, -1)
    payloads = [jnp.where((chip ^ mask) < chip, total[1], total[0]) for mask in masks]
    payloads, held = lax.optimization_barrier((payloads, per_head))
    mine = [(mask, (chip ^ mask) < chip, swap_chips(payload, mask)) for mask, payload in zip(masks, payloads)]
    near_other = swap_cores(jnp.where(core == 0, keep[0], keep[1]))
    near_mine = jnp.where(core == 0, received[1], received[0])
    local = local_part(level_table, held)

    own = lax.dynamic_slice_in_dim(weights, core * half, half, 1)[:, :, None, None]
    others = lax.dynamic_slice_in_dim(weights, (1 - core) * half, half, 1)[:, :, None, None]
    upper = (core == 1).astype(F32)
    far = []
    for table, near, pieces in (
        (own, near_mine, [piece for _, _, piece in mine]),
        (others, near_other, [swap_cores(piece) for _, _, piece in mine]),
    ):
        keys_far = upper * table[local_levels] * near
        queries_far = (1.0 - upper) * table[local_levels] * near
        for (mask, later, _), piece in zip(mine, pieces):
            term = table[local_levels + mask.bit_length()] * piece
            keys_far += jnp.where(later, term, 0.0)
            queries_far += jnp.where(later, 0.0, term)
        far.append(jnp.stack([keys_far, queries_far]))
    first = jnp.where(core == 0, far[0], far[1])
    second = jnp.where(core == 0, far[1], far[0])
    return final_part(per_head, local, jnp.concatenate([first, second], axis=1))


def solution(mesh):
    part = P(("groups", "seq", "rep"), "head", None)
    return jax.shard_map(
        per_device,
        mesh=mesh,
        in_specs=(part, part, part, part, P(None, "head")),
        out_specs=(part, part, part, part),
        check_vma=False,
    )
```

```python
import functools
import math

import jax
import jax.numpy as jnp
import numpy as np
from jax import lax
from jax.experimental import pallas as pl
from jax.experimental.pallas import tpu as pltpu
from jax.sharding import PartitionSpec as P

BLOCK = 64
TILE = 128
CHUNKS = 2
F32 = jnp.float32
BF16 = jnp.bfloat16


def swap_cores(block):
    return lax.ppermute(block, "rep", [(0, 1), (1, 0)])


def swap_chips(block, mask):
    count = lax.axis_size("seq")
    return lax.ppermute(block, "seq", [(chip, chip ^ mask) for chip in range(count)])


def level_scale(level):
    return float(np.float32(1.0) / np.sqrt(np.float32(BLOCK * 2 ** max(level - 1, 0))))


def dot_tn(left, right):
    return lax.dot_general(left, right, (((0,), (0,)), ((), ())), preferred_element_type=F32)


def dot_nt(left, right):
    return lax.dot_general(left, right, (((1,), (1,)), ((), ())), preferred_element_type=F32)


def dot_nn(left, right):
    return lax.dot_general(left, right, (((1,), (0,)), ((), ())), preferred_element_type=F32)


def split(value):
    high = value.astype(BF16)
    return high, (value - high.astype(F32)).astype(BF16)


def state_kernel(heads, q_ref, k_ref, v_ref, g_ref, send_ref, keep_ref, per_head_ref, narrow, wide, arrived):
    rows = q_ref.shape[0] // heads
    half = heads // 2
    core = lax.axis_index("rep")
    sources = (q_ref, k_ref, v_ref, g_ref)
    length = rows * heads // CHUNKS

    def fetch(which, chunk):
        span = pl.ds(chunk * length, length)
        return pltpu.make_async_copy(sources[which].at[span], narrow.at[which, span], arrived.at[which, chunk])

    pairs = ((1, 2), (0, 3))
    for pair in pairs:
        for which in pair:
            for chunk in range(CHUNKS):
                fetch(which, chunk).start()
    for kind, pair in enumerate(pairs):
        for which in pair:
            for chunk in range(CHUNKS):
                fetch(which, chunk).wait()
            wide[which] = narrow[which].astype(F32)
            for head in range(heads):
                per_head_ref[which, head] = wide[which, pl.ds(head, rows, stride=heads), :].astype(BF16)
        for place in range(half):
            for owner, out_ref in ((1 - core, send_ref), (core, keep_ref)):
                head = owner * half + place
                out_ref[kind, place] = dot_tn(per_head_ref[pair[0], head], per_head_ref[pair[1], head])


def states(heads, flat):
    rows, width = flat[0].shape[0] // heads, flat[0].shape[1]
    half = (2, heads // 2, width, width)
    return pl.pallas_call(
        functools.partial(state_kernel, heads),
        out_shape=(
            jax.ShapeDtypeStruct(half, F32),
            jax.ShapeDtypeStruct(half, F32),
            jax.ShapeDtypeStruct((4, heads, rows, width), BF16),
        ),
        in_specs=[pl.BlockSpec(memory_space=pltpu.HBM)] * 4,
        out_specs=[pl.BlockSpec(memory_space=pltpu.VMEM)] * 3,
        scratch_shapes=[
            pltpu.VMEM((4, rows * heads, width), BF16),
            pltpu.VMEM((4, rows * heads, width), F32),
            pltpu.SemaphoreType.DMA((4, CHUNKS)),
        ],
        compiler_params=pltpu.CompilerParams(vmem_limit_bytes=24 * 2**20),
        name="states",
    )(*[pltpu.with_memory_space_constraint(array, pltpu.HBM) for array in flat])


def local_kernel(chosen, table_ref, per_head_ref, *refs):
    out_ref = refs[-1]
    rows = per_head_ref.shape[2]
    for head in chosen:
        local_head(head, rows, table_ref, per_head_ref.at[:, head], out_ref.at[:, head])


def local_head(head, rows, table_ref, per_head_ref, out_ref):
    tiles = rows // TILE
    inner = (TILE // BLOCK).bit_length()
    weight = [table_ref[head, level] * level_scale(level) for level in range(inner + tiles.bit_length() - 1)]
    row = lax.broadcasted_iota(jnp.int32, (TILE, TILE), 0)
    column = lax.broadcasted_iota(jnp.int32, (TILE, TILE), 1)
    apart = jnp.bitwise_xor(row // BLOCK, column // BLOCK)
    level_mask = jnp.where(apart == 0, weight[0], weight[1])
    for level in range(2, inner):
        level_mask = jnp.where(apart >= 1 << (level - 1), weight[level], level_mask)
    lower = jnp.where(row >= column, level_mask, 0.0)
    upper = jnp.where(row <= column, level_mask, 0.0)
    part = [[per_head_ref[which, pl.ds(tile * TILE, TILE), :] for tile in range(tiles)] for which in range(4)]
    queries, keys, values, out_grad = part

    def sums(states):
        table = {(0, tile): states[tile] for tile in range(tiles)}
        for bit in range(1, tiles.bit_length() - 1):
            for group in range(tiles >> bit):
                table[bit, group] = table[bit - 1, 2 * group] + table[bit - 1, 2 * group + 1]
        return table

    def gather(table, tile, side):
        total = None
        for bit in range(tiles.bit_length() - 1):
            if (tile >> bit) % 2 == side:
                term = weight[inner + bit] * table[bit, (tile >> bit) ^ 1]
                total = term if total is None else total + term
        return [] if total is None else split(total)

    turned = [[block.T for block in array] for array in part]
    q_t, k_t, v_t, g_t = turned
    key_sums = sums([dot_nn(k_t[tile], values[tile]) for tile in range(tiles)])
    key_sums_t = sums([dot_nn(v_t[tile], keys[tile]) for tile in range(tiles)])
    query_sums = sums([dot_nn(q_t[tile], out_grad[tile]) for tile in range(tiles)])
    query_sums_t = sums([dot_nn(g_t[tile], queries[tile]) for tile in range(tiles)])
    held = []
    for tile in range(tiles):
        q, k, v, g = (array[tile] for array in part)
        terms = (
            (dot_nn(q, k_t[tile]) * lower, v, q, gather(key_sums, tile, 1)),
            (dot_nn(g, v_t[tile]) * lower, k, g, gather(key_sums_t, tile, 1)),
            (dot_nn(v, g_t[tile]) * upper, q, v, gather(query_sums_t, tile, 0)),
            (dot_nn(k, q_t[tile]) * upper, g, k, gather(query_sums, tile, 0)),
        )
        held.append(terms)
    for tile in range(tiles):
        for which, (inside, other, mine, pieces) in enumerate(held[tile]):
            result = dot_nn(jnp.concatenate([*split(inside), *([mine, mine] if pieces else [])], 1), jnp.concatenate([other, other, *pieces], 0))
            out_ref[which, pl.ds(tile * TILE, TILE), :] = result


def local_part(chosen, flops, table, per_head, *earlier):
    vmem = pl.BlockSpec(memory_space=pltpu.VMEM)
    return pl.pallas_call(
        functools.partial(local_kernel, chosen),
        out_shape=jax.ShapeDtypeStruct(per_head.shape, F32),
        in_specs=[pl.BlockSpec(memory_space=pltpu.SMEM)] + [vmem] * (1 + len(earlier)),
        out_specs=vmem,
        input_output_aliases={2: 0} if earlier else {},
        compiler_params=pltpu.CompilerParams(vmem_limit_bytes=16 * 2**20),
        cost_estimate=pl.CostEstimate(flops=flops, bytes_accessed=flops // 1000, transcendentals=0),
        name="local",
    )(table, per_head, *earlier)


def far_states(table_ref, head, rows, near, pair, groups):
    core, chip = lax.axis_index("rep"), lax.axis_index("seq")
    terms = [(core == 1, near), (chip % 2 == 1, pair)]
    terms += [((chip >> bit) % 2 == 1, group) for bit, group in enumerate(groups, 1)]
    keys_far = queries_far = 0.0
    for level, (later, piece) in enumerate(terms, (rows // BLOCK).bit_length()):
        weight = table_ref[head, level] * level_scale(level)
        keys_far += jnp.where(later, weight, 0.0) * piece
        queries_far += jnp.where(later, 0.0, weight) * piece
    return [jnp.concatenate(split(state), 0) for state in (keys_far, keys_far.T, queries_far.T, queries_far)]


def far_heads(owner, table_ref, per_head_ref, local_ref, near, pair_ref, group_ref, wide_ref, finish=None):
    heads, rows = per_head_ref.shape[1:3]
    half = heads // 2
    chosen = [owner * half + place for place in range(half)]
    states = [
        far_states(table_ref, head, rows, near(place), pair_ref[place], [group_ref[place, bit] for bit in range(group_ref.shape[1])])
        for place, head in enumerate(chosen)
    ]
    for which, source in enumerate((0, 3, 2, 1)):
        for head, pieces in zip(chosen, states):
            mine = per_head_ref[source, head]
            result = local_ref[which, head] + dot_nn(jnp.concatenate([mine, mine], 1), pieces[which])
            wide_ref[which, pl.ds(head, rows, stride=heads), :] = result
        if finish is not None:
            finish(which)


def own_kernel(table_ref, per_head_ref, local_ref, received_ref, pair_ref, group_ref, wide_ref):
    core = lax.axis_index("rep")
    far_heads(core, table_ref, per_head_ref, local_ref, lambda place: received_ref[1 - core, place],
              pair_ref, group_ref, wide_ref)


def last_kernel(table_ref, per_head_ref, local_ref, near_ref, pair_ref, group_ref, _, *refs):
    out_refs, (wide_ref, narrow, left) = refs[:4], refs[4:]
    copies = []

    def finish(which):
        narrow[which] = wide_ref[which].astype(BF16)
        copy = pltpu.make_async_copy(narrow.at[which], out_refs[which], left.at[which])
        copy.start()
        copies.append(copy)

    far_heads(1 - lax.axis_index("rep"), table_ref, per_head_ref, local_ref, lambda place: near_ref[place],
              pair_ref, group_ref, wide_ref, finish)
    for copy in copies:
        copy.wait()


def own_part(table, per_head, *operands):
    _, heads, rows, width = per_head.shape
    vmem = pl.BlockSpec(memory_space=pltpu.VMEM)
    return pl.pallas_call(
        own_kernel,
        out_shape=jax.ShapeDtypeStruct((4, rows * heads, width), F32),
        in_specs=[pl.BlockSpec(memory_space=pltpu.SMEM)] + [vmem] * (1 + len(operands)),
        out_specs=vmem,
        compiler_params=pltpu.CompilerParams(vmem_limit_bytes=16 * 2**20),
        cost_estimate=pl.CostEstimate(flops=10**9, bytes_accessed=3 * 2**20, transcendentals=0),
        name="own",
    )(table, per_head, *operands)


def last_part(table, per_head, *operands):
    _, heads, rows, width = per_head.shape
    vmem = pl.BlockSpec(memory_space=pltpu.VMEM)
    wide = operands[-1]
    outs = pl.pallas_call(
        last_kernel,
        out_shape=[jax.ShapeDtypeStruct((rows * heads, width), BF16)] * 4 + [jax.ShapeDtypeStruct(wide.shape, F32)],
        in_specs=[pl.BlockSpec(memory_space=pltpu.SMEM)] + [vmem] * (1 + len(operands)),
        out_specs=[pl.BlockSpec(memory_space=pltpu.HBM)] * 4 + [vmem],
        scratch_shapes=[pltpu.VMEM((4, rows * heads, width), BF16), pltpu.SemaphoreType.DMA((4,))],
        input_output_aliases={1 + len(operands): 4},
        compiler_params=pltpu.CompilerParams(vmem_limit_bytes=16 * 2**20),
        name="last",
    )(table, per_head, *operands)
    return tuple(out.reshape(rows, heads, width) for out in outs[:4])


def load_kernel(keep_ref, received_ref, pair_ref, rest_ref, near_ref):
    core, chip = lax.axis_index("rep"), lax.axis_index("seq")
    kind = chip % 2
    pair_ref[...] = keep_ref[kind] + received_ref[kind]
    for bit in range(rest_ref.shape[0]):
        kind = (chip >> (bit + 1)) % 2
        rest_ref[bit] = keep_ref[kind, 1] + received_ref[kind, 1]
    near_ref[...] = keep_ref[core]


def loads_of(bits, keep, received):
    vmem = pl.BlockSpec(memory_space=pltpu.VMEM)
    half, width = keep.shape[1], keep.shape[2]
    shapes = ((half, width, width), (bits - 1, width, width), (half, width, width))
    return pl.pallas_call(
        load_kernel,
        out_shape=[jax.ShapeDtypeStruct(shape, F32) for shape in shapes],
        in_specs=[vmem] * 2,
        out_specs=[vmem] * 3,
        compiler_params=pltpu.CompilerParams(vmem_limit_bytes=4 * 2**20),
        cost_estimate=pl.CostEstimate(flops=10**9, bytes_accessed=3 * 2**20, transcendentals=0),
        name="loads",
    )(keep, received)


def per_device(queries, keys, values, out_grad, level_table):
    rows, heads, width = queries.shape
    half = heads // 2
    bits = lax.axis_size("seq").bit_length() - 1
    chip = lax.axis_index("seq")
    table = level_table.T
    flat = [array.reshape(rows * heads, width) for array in (queries, keys, values, out_grad)]
    send, keep, per_head = states(heads, flat)
    received = swap_cores(send)
    first = [
        jnp.where((chip >> bit) % 2 == 1, keep[1, 0] + received[1, 0], keep[0, 0] + received[0, 0])
        for bit in range(1, bits)
    ]
    first, keep, received = lax.optimization_barrier((first, keep, received))
    half_way = [
        sum(swap_chips(first[bit - 1], mask) for mask in range(1 << bit, 2 << bit, 2)) for bit in range(1, bits)
    ]
    pair_load, rest, near_load = loads_of(bits, keep, received)
    pair_load, rest, near_load, held = lax.optimization_barrier((pair_load, rest, near_load, per_head))
    group_b = [
        [swap_chips(rest[bit - 1], mask) for mask in range((2 << bit) - 1, (1 << bit) - 1, -1)] for bit in range(1, bits)
    ]
    pair = swap_chips(pair_load, 1)
    near = swap_cores(near_load)
    local_a = local_part((0,), 1000, table, held)
    half_way = jnp.stack(half_way)
    half_way, held, local_a = lax.optimization_barrier((half_way, held, local_a))
    hop = swap_chips(half_way, 1)
    local_b = local_part(tuple(range(1, heads)), 10**9, table, held, local_a)
    pair, hop, group_b, local_b = lax.optimization_barrier((pair, hop, group_b, local_b))
    pair_o = swap_cores(pair)
    group = jnp.stack([half_way + hop, jnp.stack([sum(pieces) for pieces in group_b])])
    group_o = swap_cores(group)
    wide = own_part(table, per_head, local_b, received, pair, group)
    return last_part(table, per_head, local_b, near, pair_o, group_o, wide)


def solution(mesh):
    part = P(("groups", "seq", "rep"), "head", None)
    return jax.shard_map(
        per_device,
        mesh=mesh,
        in_specs=(part, part, part, part, P(None, "head")),
        out_specs=(part, part, part, part),
        check_vma=False,
    )
```

```python
import functools
import math

import jax
import jax.numpy as jnp
import numpy as np
from jax import lax
from jax.experimental import pallas as pl
from jax.experimental.pallas import tpu as pltpu
from jax.sharding import PartitionSpec as P

BLOCK = 64
TILE = 128
CHUNKS = 2
F32 = jnp.float32
BF16 = jnp.bfloat16


def swap_cores(block):
    return lax.ppermute(block, "rep", [(0, 1), (1, 0)])


def swap_chips(block, mask):
    count = lax.axis_size("seq")
    return lax.ppermute(block, "seq", [(chip, chip ^ mask) for chip in range(count)])


def level_scale(level):
    return float(np.float32(1.0) / np.sqrt(np.float32(BLOCK * 2 ** max(level - 1, 0))))


def weight_of(table_ref, head, level):
    return table_ref[pl.ds(head, 1), level : level + 1] * level_scale(level)


def dot_tn(left, right):
    return lax.dot_general(left, right, (((0,), (0,)), ((), ())), preferred_element_type=F32)


def dot_nt(left, right):
    return lax.dot_general(left, right, (((1,), (1,)), ((), ())), preferred_element_type=F32)


def dot_nn(left, right):
    return lax.dot_general(left, right, (((1,), (0,)), ((), ())), preferred_element_type=F32)


def split(value):
    high = value.astype(BF16)
    return high, (value - high.astype(F32)).astype(BF16)


def state_kernel(heads, q_ref, k_ref, v_ref, g_ref, send_ref, keep_ref, per_head_ref, narrow, wide, arrived):
    rows = q_ref.shape[0] // heads
    half = heads // 2
    core = lax.axis_index("rep")
    sources = (q_ref, k_ref, v_ref, g_ref)
    length = rows * heads // CHUNKS

    def fetch(which, chunk):
        span = pl.ds(chunk * length, length)
        return pltpu.make_async_copy(sources[which].at[span], narrow.at[which, span], arrived.at[which, chunk])

    pairs = ((1, 2), (0, 3))
    for pair in pairs:
        for which in pair:
            for chunk in range(CHUNKS):
                fetch(which, chunk).start()
    for kind, pair in enumerate(pairs):
        for which in pair:
            for chunk in range(CHUNKS):
                fetch(which, chunk).wait()
            wide[which] = narrow[which].astype(F32)
            for head in range(heads):
                per_head_ref[which, head] = wide[which, pl.ds(head, rows, stride=heads), :].astype(BF16)
        for place in range(half):
            for owner, out_ref in ((1 - core, send_ref), (core, keep_ref)):
                head = owner * half + place
                out_ref[kind, place] = dot_tn(per_head_ref[pair[0], head], per_head_ref[pair[1], head])


def states(heads, flat):
    rows, width = flat[0].shape[0] // heads, flat[0].shape[1]
    half = (2, heads // 2, width, width)
    return pl.pallas_call(
        functools.partial(state_kernel, heads),
        out_shape=(
            jax.ShapeDtypeStruct(half, F32),
            jax.ShapeDtypeStruct(half, F32),
            jax.ShapeDtypeStruct((4, heads, rows, width), BF16),
        ),
        in_specs=[pl.BlockSpec(memory_space=pltpu.HBM)] * 4,
        out_specs=[pl.BlockSpec(memory_space=pltpu.VMEM)] * 3,
        scratch_shapes=[
            pltpu.VMEM((4, rows * heads, width), BF16),
            pltpu.VMEM((4, rows * heads, width), F32),
            pltpu.SemaphoreType.DMA((4, CHUNKS)),
        ],
        compiler_params=pltpu.CompilerParams(vmem_limit_bytes=24 * 2**20),
        name="states",
    )(*[pltpu.with_memory_space_constraint(array, pltpu.HBM) for array in flat])


def local_kernel(chosen, table_ref, per_head_ref, *refs):
    out_ref = refs[-1]
    rows = per_head_ref.shape[2]
    for head in chosen:
        local_head(head, rows, table_ref, per_head_ref.at[:, head], out_ref.at[:, head])


def local_head(head, rows, table_ref, per_head_ref, out_ref):
    tiles = rows // TILE
    inner = (TILE // BLOCK).bit_length()
    weight = [weight_of(table_ref, head, level) for level in range(inner + tiles.bit_length() - 1)]
    row = lax.broadcasted_iota(jnp.int32, (TILE, TILE), 0)
    column = lax.broadcasted_iota(jnp.int32, (TILE, TILE), 1)
    apart = jnp.bitwise_xor(row // BLOCK, column // BLOCK)
    level_mask = jnp.where(apart == 0, weight[0], weight[1])
    for level in range(2, inner):
        level_mask = jnp.where(apart >= 1 << (level - 1), weight[level], level_mask)
    lower = jnp.where(row >= column, level_mask, 0.0)
    upper = jnp.where(row <= column, level_mask, 0.0)
    part = [[per_head_ref[which, pl.ds(tile * TILE, TILE), :] for tile in range(tiles)] for which in range(4)]
    queries, keys, values, out_grad = part

    def sums(states):
        table = {(0, tile): states[tile] for tile in range(tiles)}
        for bit in range(1, tiles.bit_length() - 1):
            for group in range(tiles >> bit):
                table[bit, group] = table[bit - 1, 2 * group] + table[bit - 1, 2 * group + 1]
        return table

    def gather(table, tile, side):
        total = None
        for bit in range(tiles.bit_length() - 1):
            if (tile >> bit) % 2 == side:
                term = weight[inner + bit] * table[bit, (tile >> bit) ^ 1]
                total = term if total is None else total + term
        return [] if total is None else split(total)

    turned = [[block.T for block in array] for array in part]
    q_t, k_t, v_t, g_t = turned
    key_sums = sums([dot_nn(k_t[tile], values[tile]) for tile in range(tiles)])
    key_sums_t = sums([dot_nn(v_t[tile], keys[tile]) for tile in range(tiles)])
    query_sums = sums([dot_nn(q_t[tile], out_grad[tile]) for tile in range(tiles)])
    query_sums_t = sums([dot_nn(g_t[tile], queries[tile]) for tile in range(tiles)])
    held = []
    for tile in range(tiles):
        q, k, v, g = (array[tile] for array in part)
        terms = (
            (dot_nn(q, k_t[tile]) * lower, v, q, gather(key_sums, tile, 1)),
            (dot_nn(g, v_t[tile]) * lower, k, g, gather(key_sums_t, tile, 1)),
            (dot_nn(v, g_t[tile]) * upper, q, v, gather(query_sums_t, tile, 0)),
            (dot_nn(k, q_t[tile]) * upper, g, k, gather(query_sums, tile, 0)),
        )
        held.append(terms)
    for tile in range(tiles):
        for which, (inside, other, mine, pieces) in enumerate(held[tile]):
            result = dot_nn(jnp.concatenate([*split(inside), *([mine, mine] if pieces else [])], 1), jnp.concatenate([other, other, *pieces], 0))
            out_ref[which, pl.ds(tile * TILE, TILE), :] = result


def local_part(chosen, flops, table, per_head, *earlier):
    vmem = pl.BlockSpec(memory_space=pltpu.VMEM)
    return pl.pallas_call(
        functools.partial(local_kernel, chosen),
        out_shape=jax.ShapeDtypeStruct(per_head.shape, F32),
        in_specs=[pl.BlockSpec(memory_space=pltpu.VMEM)] + [vmem] * (1 + len(earlier)),
        out_specs=vmem,
        input_output_aliases={2: 0} if earlier else {},
        compiler_params=pltpu.CompilerParams(vmem_limit_bytes=16 * 2**20),
        cost_estimate=pl.CostEstimate(flops=flops, bytes_accessed=flops // 1000, transcendentals=0),
        name="local",
    )(table, per_head, *earlier)


def far_states(table_ref, head, rows, near, pair, groups):
    core, chip = lax.axis_index("rep"), lax.axis_index("seq")
    terms = [(core == 1, near), (chip % 2 == 1, pair)]
    terms += [((chip >> bit) % 2 == 1, group) for bit, group in enumerate(groups, 1)]
    keys_far = queries_far = 0.0
    for level, (later, piece) in enumerate(terms, (rows // BLOCK).bit_length()):
        weight = weight_of(table_ref, head, level)
        keys_far += jnp.where(later, weight, 0.0) * piece
        queries_far += jnp.where(later, 0.0, weight) * piece
    return [jnp.concatenate(split(state), 0) for state in (keys_far, keys_far.T, queries_far.T, queries_far)]


def far_heads(owner, table_ref, per_head_ref, local_ref, near, pair_ref, group_ref, wide_ref, finish=None):
    heads, rows = per_head_ref.shape[1:3]
    half = heads // 2
    chosen = [owner * half + place for place in range(half)]
    states = [
        far_states(table_ref, head, rows, near(place), pair_ref[place], [group_ref[place, bit] for bit in range(group_ref.shape[1])])
        for place, head in enumerate(chosen)
    ]
    for which, source in enumerate((0, 3, 2, 1)):
        for head, pieces in zip(chosen, states):
            mine = per_head_ref[source, head]
            result = local_ref[which, head] + dot_nn(jnp.concatenate([mine, mine], 1), pieces[which])
            wide_ref[which, pl.ds(head, rows, stride=heads), :] = result
        if finish is not None:
            finish(which)


def own_kernel(table_ref, per_head_ref, local_ref, received_ref, pair_ref, group_ref, wide_ref):
    core = lax.axis_index("rep")
    far_heads(core, table_ref, per_head_ref, local_ref, lambda place: received_ref[1 - core, place],
              pair_ref, group_ref, wide_ref)


def last_kernel(table_ref, per_head_ref, local_ref, near_ref, pair_ref, group_ref, _, *refs):
    out_refs, (wide_ref, narrow, left) = refs[:4], refs[4:]
    copies = []

    def finish(which):
        narrow[which] = wide_ref[which].astype(BF16)
        copy = pltpu.make_async_copy(narrow.at[which], out_refs[which], left.at[which])
        copy.start()
        copies.append(copy)

    far_heads(1 - lax.axis_index("rep"), table_ref, per_head_ref, local_ref, lambda place: near_ref[place],
              pair_ref, group_ref, wide_ref, finish)
    for copy in copies:
        copy.wait()


def own_part(table, per_head, *operands):
    _, heads, rows, width = per_head.shape
    vmem = pl.BlockSpec(memory_space=pltpu.VMEM)
    return pl.pallas_call(
        own_kernel,
        out_shape=jax.ShapeDtypeStruct((4, rows * heads, width), F32),
        in_specs=[pl.BlockSpec(memory_space=pltpu.VMEM)] + [vmem] * (1 + len(operands)),
        out_specs=vmem,
        compiler_params=pltpu.CompilerParams(vmem_limit_bytes=16 * 2**20),
        cost_estimate=pl.CostEstimate(flops=10**9, bytes_accessed=3 * 2**20, transcendentals=0),
        name="own",
    )(table, per_head, *operands)


def last_part(table, per_head, *operands):
    _, heads, rows, width = per_head.shape
    vmem = pl.BlockSpec(memory_space=pltpu.VMEM)
    wide = operands[-1]
    outs = pl.pallas_call(
        last_kernel,
        out_shape=[jax.ShapeDtypeStruct((rows * heads, width), BF16)] * 4 + [jax.ShapeDtypeStruct(wide.shape, F32)],
        in_specs=[pl.BlockSpec(memory_space=pltpu.VMEM)] + [vmem] * (1 + len(operands)),
        out_specs=[pl.BlockSpec(memory_space=pltpu.HBM)] * 4 + [vmem],
        scratch_shapes=[pltpu.VMEM((4, rows * heads, width), BF16), pltpu.SemaphoreType.DMA((4,))],
        input_output_aliases={1 + len(operands): 4},
        compiler_params=pltpu.CompilerParams(vmem_limit_bytes=16 * 2**20),
        name="last",
    )(table, per_head, *operands)
    return tuple(out.reshape(rows, heads, width) for out in outs[:4])


def load_kernel(keep_ref, received_ref, pair_ref, rest_ref, near_ref):
    core, chip = lax.axis_index("rep"), lax.axis_index("seq")
    kind = chip % 2
    pair_ref[...] = keep_ref[kind] + received_ref[kind]
    for bit in range(rest_ref.shape[0]):
        kind = (chip >> (bit + 1)) % 2
        rest_ref[bit] = keep_ref[kind, 1] + received_ref[kind, 1]
    near_ref[...] = keep_ref[core]


def loads_of(bits, keep, received):
    vmem = pl.BlockSpec(memory_space=pltpu.VMEM)
    half, width = keep.shape[1], keep.shape[2]
    shapes = ((half, width, width), (bits - 1, width, width), (half, width, width))
    return pl.pallas_call(
        load_kernel,
        out_shape=[jax.ShapeDtypeStruct(shape, F32) for shape in shapes],
        in_specs=[vmem] * 2,
        out_specs=[vmem] * 3,
        compiler_params=pltpu.CompilerParams(vmem_limit_bytes=4 * 2**20),
        cost_estimate=pl.CostEstimate(flops=10**9, bytes_accessed=3 * 2**20, transcendentals=0),
        name="loads",
    )(keep, received)


def per_device(queries, keys, values, out_grad, level_table):
    rows, heads, width = queries.shape
    half = heads // 2
    bits = lax.axis_size("seq").bit_length() - 1
    chip = lax.axis_index("seq")
    table = level_table.T
    flat = [array.reshape(rows * heads, width) for array in (queries, keys, values, out_grad)]
    send, keep, per_head = states(heads, flat)
    received = swap_cores(send)
    first = [
        jnp.where((chip >> bit) % 2 == 1, keep[1, 0] + received[1, 0], keep[0, 0] + received[0, 0])
        for bit in range(1, bits)
    ]
    first, keep, received = lax.optimization_barrier((first, keep, received))
    half_way = [
        sum(swap_chips(first[bit - 1], mask) for mask in range(1 << bit, 2 << bit, 2)) for bit in range(1, bits)
    ]
    pair_load, rest, near_load = loads_of(bits, keep, received)
    pair_load, rest, near_load, held = lax.optimization_barrier((pair_load, rest, near_load, per_head))
    group_b = [
        [swap_chips(rest[bit - 1], mask) for mask in range((2 << bit) - 1, (1 << bit) - 1, -1)] for bit in range(1, bits)
    ]
    pair = swap_chips(pair_load, 1)
    near = swap_cores(near_load)
    local_a = local_part((0,), 1000, table, held)
    half_way = jnp.stack(half_way)
    half_way, held, local_a = lax.optimization_barrier((half_way, held, local_a))
    hop = swap_chips(half_way, 1)
    local_b = local_part(tuple(range(1, heads)), 10**9, table, held, local_a)
    pair, hop, group_b, local_b = lax.optimization_barrier((pair, hop, group_b, local_b))
    pair_o = swap_cores(pair)
    group = jnp.stack([half_way + hop, jnp.stack([sum(pieces) for pieces in group_b])])
    group_o = swap_cores(group)
    wide = own_part(table, per_head, local_b, received, pair, group)
    return last_part(table, per_head, local_b, near, pair_o, group_o, wide)


def solution(mesh):
    part = P(("groups", "seq", "rep"), "head", None)
    return jax.shard_map(
        per_device,
        mesh=mesh,
        in_specs=(part, part, part, part, P(None, "head")),
        out_specs=(part, part, part, part),
        check_vma=False,
    )
```

```python
import functools
import math

import jax
import jax.numpy as jnp
import numpy as np
from jax import lax
from jax.experimental import pallas as pl
from jax.experimental.pallas import tpu as pltpu
from jax.sharding import PartitionSpec as P

BLOCK = 64
TILE = 128
CHUNKS = 2
F32 = jnp.float32
BF16 = jnp.bfloat16


def swap_cores(block):
    return lax.ppermute(block, "rep", [(0, 1), (1, 0)])


def swap_chips(block, mask):
    count = lax.axis_size("seq")
    return lax.ppermute(block, "seq", [(chip, chip ^ mask) for chip in range(count)])


def level_scale(level):
    return float(np.float32(1.0) / np.sqrt(np.float32(BLOCK * 2 ** max(level - 1, 0))))


def weight_of(table_ref, head, level):
    return table_ref[pl.ds(head, 1), level : level + 1] * level_scale(level)


def dot_tn(left, right):
    return lax.dot_general(left, right, (((0,), (0,)), ((), ())), preferred_element_type=F32)


def dot_nt(left, right):
    return lax.dot_general(left, right, (((1,), (1,)), ((), ())), preferred_element_type=F32)


def dot_nn(left, right):
    return lax.dot_general(left, right, (((1,), (0,)), ((), ())), preferred_element_type=F32)


def split(value):
    high = value.astype(BF16)
    return high, (value - high.astype(F32)).astype(BF16)


def state_kernel(
    heads, q_ref, k_ref, v_ref, g_ref, levels_ref, send_ref, keep_ref, per_head_ref, table_ref, narrow, wide, arrived, listed
):
    rows = q_ref.shape[0] // heads
    half = heads // 2
    core = lax.axis_index("rep")
    sources = (q_ref, k_ref, v_ref, g_ref)
    length = rows * heads // CHUNKS

    def fetch(which, chunk):
        span = pl.ds(chunk * length, length)
        return pltpu.make_async_copy(sources[which].at[span], narrow.at[which, span], arrived.at[which, chunk])

    pairs = ((1, 2), (0, 3))
    for pair in pairs:
        for which in pair:
            for chunk in range(CHUNKS):
                fetch(which, chunk).start()
    table = pltpu.make_async_copy(levels_ref, table_ref, listed)
    table.start()
    for kind, pair in enumerate(pairs):
        for which in pair:
            for chunk in range(CHUNKS):
                fetch(which, chunk).wait()
            wide[which] = narrow[which].astype(F32)
            for head in range(heads):
                per_head_ref[which, head] = wide[which, pl.ds(head, rows, stride=heads), :].astype(BF16)
        for place in range(half):
            for owner, out_ref in ((1 - core, send_ref), (core, keep_ref)):
                head = owner * half + place
                out_ref[kind, place] = dot_tn(per_head_ref[pair[0], head], per_head_ref[pair[1], head])
    table.wait()


def states(flat, table):
    heads = table.shape[0]
    rows, width = flat[0].shape[0] // heads, flat[0].shape[1]
    half = (2, heads // 2, width, width)
    return pl.pallas_call(
        functools.partial(state_kernel, heads),
        out_shape=(
            jax.ShapeDtypeStruct(half, F32),
            jax.ShapeDtypeStruct(half, F32),
            jax.ShapeDtypeStruct((4, heads, rows, width), BF16),
            jax.ShapeDtypeStruct(table.shape, F32),
        ),
        in_specs=[pl.BlockSpec(memory_space=pltpu.HBM)] * 5,
        out_specs=[pl.BlockSpec(memory_space=pltpu.VMEM)] * 4,
        scratch_shapes=[
            pltpu.VMEM((4, rows * heads, width), BF16),
            pltpu.VMEM((4, rows * heads, width), F32),
            pltpu.SemaphoreType.DMA((4, CHUNKS)),
            pltpu.SemaphoreType.DMA,
        ],
        compiler_params=pltpu.CompilerParams(vmem_limit_bytes=24 * 2**20),
        name="states",
    )(*[pltpu.with_memory_space_constraint(array, pltpu.HBM) for array in (*flat, table)])


def local_kernel(chosen, table_ref, per_head_ref, *refs):
    out_ref = refs[-1]
    rows = per_head_ref.shape[2]
    for head in chosen:
        local_head(head, rows, table_ref, per_head_ref.at[:, head], out_ref.at[:, head])


def local_head(head, rows, table_ref, per_head_ref, out_ref):
    tiles = rows // TILE
    inner = (TILE // BLOCK).bit_length()
    weight = [weight_of(table_ref, head, level) for level in range(inner + tiles.bit_length() - 1)]
    row = lax.broadcasted_iota(jnp.int32, (TILE, TILE), 0)
    column = lax.broadcasted_iota(jnp.int32, (TILE, TILE), 1)
    apart = jnp.bitwise_xor(row // BLOCK, column // BLOCK)
    level_mask = jnp.where(apart == 0, weight[0], weight[1])
    for level in range(2, inner):
        level_mask = jnp.where(apart >= 1 << (level - 1), weight[level], level_mask)
    lower = jnp.where(row >= column, level_mask, 0.0)
    upper = jnp.where(row <= column, level_mask, 0.0)
    part = [[per_head_ref[which, pl.ds(tile * TILE, TILE), :] for tile in range(tiles)] for which in range(4)]
    queries, keys, values, out_grad = part

    def sums(states):
        table = {(0, tile): states[tile] for tile in range(tiles)}
        for bit in range(1, tiles.bit_length() - 1):
            for group in range(tiles >> bit):
                table[bit, group] = table[bit - 1, 2 * group] + table[bit - 1, 2 * group + 1]
        return table

    def gather(table, tile, side):
        total = None
        for bit in range(tiles.bit_length() - 1):
            if (tile >> bit) % 2 == side:
                term = weight[inner + bit] * table[bit, (tile >> bit) ^ 1]
                total = term if total is None else total + term
        return [] if total is None else split(total)

    turned = [[block.T for block in array] for array in part]
    q_t, k_t, v_t, g_t = turned
    key_sums = sums([dot_nn(k_t[tile], values[tile]) for tile in range(tiles)])
    key_sums_t = sums([dot_nn(v_t[tile], keys[tile]) for tile in range(tiles)])
    query_sums = sums([dot_nn(q_t[tile], out_grad[tile]) for tile in range(tiles)])
    query_sums_t = sums([dot_nn(g_t[tile], queries[tile]) for tile in range(tiles)])
    held = []
    for tile in range(tiles):
        q, k, v, g = (array[tile] for array in part)
        terms = (
            (dot_nn(q, k_t[tile]) * lower, v, q, gather(key_sums, tile, 1)),
            (dot_nn(g, v_t[tile]) * lower, k, g, gather(key_sums_t, tile, 1)),
            (dot_nn(v, g_t[tile]) * upper, q, v, gather(query_sums_t, tile, 0)),
            (dot_nn(k, q_t[tile]) * upper, g, k, gather(query_sums, tile, 0)),
        )
        held.append(terms)
    for tile in range(tiles):
        for which, (inside, other, mine, pieces) in enumerate(held[tile]):
            result = dot_nn(jnp.concatenate([*split(inside), *([mine, mine] if pieces else [])], 1), jnp.concatenate([other, other, *pieces], 0))
            out_ref[which, pl.ds(tile * TILE, TILE), :] = result


def local_part(chosen, flops, table, per_head, *earlier):
    vmem = pl.BlockSpec(memory_space=pltpu.VMEM)
    return pl.pallas_call(
        functools.partial(local_kernel, chosen),
        out_shape=jax.ShapeDtypeStruct(per_head.shape, F32),
        in_specs=[pl.BlockSpec(memory_space=pltpu.VMEM)] + [vmem] * (1 + len(earlier)),
        out_specs=vmem,
        input_output_aliases={2: 0} if earlier else {},
        compiler_params=pltpu.CompilerParams(vmem_limit_bytes=16 * 2**20),
        cost_estimate=pl.CostEstimate(flops=flops, bytes_accessed=flops // 1000, transcendentals=0),
        name="local",
    )(table, per_head, *earlier)


def far_states(table_ref, head, rows, near, pair, groups):
    core, chip = lax.axis_index("rep"), lax.axis_index("seq")
    terms = [(core == 1, near), (chip % 2 == 1, pair)]
    terms += [((chip >> bit) % 2 == 1, group) for bit, group in enumerate(groups, 1)]
    keys_far = queries_far = 0.0
    for level, (later, piece) in enumerate(terms, (rows // BLOCK).bit_length()):
        weight = weight_of(table_ref, head, level)
        keys_far += jnp.where(later, weight, 0.0) * piece
        queries_far += jnp.where(later, 0.0, weight) * piece
    return [jnp.concatenate(split(state), 0) for state in (keys_far, keys_far.T, queries_far.T, queries_far)]


def far_heads(owner, table_ref, per_head_ref, local_ref, near, pair_ref, group_ref, wide_ref, finish=None):
    heads, rows = per_head_ref.shape[1:3]
    half = heads // 2
    chosen = [owner * half + place for place in range(half)]
    states = [
        far_states(table_ref, head, rows, near(place), pair_ref[place], [group_ref[place, bit] for bit in range(group_ref.shape[1])])
        for place, head in enumerate(chosen)
    ]
    for which, source in enumerate((0, 3, 2, 1)):
        for head, pieces in zip(chosen, states):
            mine = per_head_ref[source, head]
            result = local_ref[which, head] + dot_nn(jnp.concatenate([mine, mine], 1), pieces[which])
            wide_ref[which, pl.ds(head, rows, stride=heads), :] = result
        if finish is not None:
            finish(which)


def own_kernel(table_ref, per_head_ref, local_ref, received_ref, pair_ref, group_ref, wide_ref):
    core = lax.axis_index("rep")
    far_heads(core, table_ref, per_head_ref, local_ref, lambda place: received_ref[1 - core, place],
              pair_ref, group_ref, wide_ref)


def last_kernel(table_ref, per_head_ref, local_ref, near_ref, pair_ref, group_ref, _, *refs):
    out_refs, (wide_ref, narrow, left) = refs[:4], refs[4:]
    copies = []

    def finish(which):
        narrow[which] = wide_ref[which].astype(BF16)
        copy = pltpu.make_async_copy(narrow.at[which], out_refs[which], left.at[which])
        copy.start()
        copies.append(copy)

    far_heads(1 - lax.axis_index("rep"), table_ref, per_head_ref, local_ref, lambda place: near_ref[place],
              pair_ref, group_ref, wide_ref, finish)
    for copy in copies:
        copy.wait()


def own_part(table, per_head, *operands):
    _, heads, rows, width = per_head.shape
    vmem = pl.BlockSpec(memory_space=pltpu.VMEM)
    return pl.pallas_call(
        own_kernel,
        out_shape=jax.ShapeDtypeStruct((4, rows * heads, width), F32),
        in_specs=[pl.BlockSpec(memory_space=pltpu.VMEM)] + [vmem] * (1 + len(operands)),
        out_specs=vmem,
        compiler_params=pltpu.CompilerParams(vmem_limit_bytes=16 * 2**20),
        cost_estimate=pl.CostEstimate(flops=10**9, bytes_accessed=3 * 2**20, transcendentals=0),
        name="own",
    )(table, per_head, *operands)


def last_part(table, per_head, *operands):
    _, heads, rows, width = per_head.shape
    vmem = pl.BlockSpec(memory_space=pltpu.VMEM)
    wide = operands[-1]
    outs = pl.pallas_call(
        last_kernel,
        out_shape=[jax.ShapeDtypeStruct((rows * heads, width), BF16)] * 4 + [jax.ShapeDtypeStruct(wide.shape, F32)],
        in_specs=[pl.BlockSpec(memory_space=pltpu.VMEM)] + [vmem] * (1 + len(operands)),
        out_specs=[pl.BlockSpec(memory_space=pltpu.HBM)] * 4 + [vmem],
        scratch_shapes=[pltpu.VMEM((4, rows * heads, width), BF16), pltpu.SemaphoreType.DMA((4,))],
        input_output_aliases={1 + len(operands): 4},
        compiler_params=pltpu.CompilerParams(vmem_limit_bytes=16 * 2**20),
        name="last",
    )(table, per_head, *operands)
    return tuple(out.reshape(rows, heads, width) for out in outs[:4])


def load_kernel(keep_ref, received_ref, pair_ref, rest_ref, near_ref):
    core, chip = lax.axis_index("rep"), lax.axis_index("seq")
    kind = chip % 2
    pair_ref[...] = keep_ref[kind] + received_ref[kind]
    for bit in range(rest_ref.shape[0]):
        kind = (chip >> (bit + 1)) % 2
        rest_ref[bit] = keep_ref[kind, 1] + received_ref[kind, 1]
    near_ref[...] = keep_ref[core]


def loads_of(bits, keep, received):
    vmem = pl.BlockSpec(memory_space=pltpu.VMEM)
    half, width = keep.shape[1], keep.shape[2]
    shapes = ((half, width, width), (bits - 1, width, width), (half, width, width))
    return pl.pallas_call(
        load_kernel,
        out_shape=[jax.ShapeDtypeStruct(shape, F32) for shape in shapes],
        in_specs=[vmem] * 2,
        out_specs=[vmem] * 3,
        compiler_params=pltpu.CompilerParams(vmem_limit_bytes=4 * 2**20),
        cost_estimate=pl.CostEstimate(flops=10**9, bytes_accessed=3 * 2**20, transcendentals=0),
        name="loads",
    )(keep, received)


def per_device(queries, keys, values, out_grad, level_table):
    rows, heads, width = queries.shape
    half = heads // 2
    bits = lax.axis_size("seq").bit_length() - 1
    chip = lax.axis_index("seq")
    flat = [array.reshape(rows * heads, width) for array in (queries, keys, values, out_grad)]
    send, keep, per_head, table = states(flat, level_table.T)
    received = swap_cores(send)
    local_a = local_part((0,), 10**9, table, per_head)
    received, per_head, local_a = lax.optimization_barrier((received, per_head, local_a))
    first = [
        jnp.where((chip >> bit) % 2 == 1, keep[1, 0] + received[1, 0], keep[0, 0] + received[0, 0])
        for bit in range(1, bits)
    ]
    first, keep, received = lax.optimization_barrier((first, keep, received))
    half_way = [
        sum(swap_chips(first[bit - 1], mask) for mask in range(1 << bit, 2 << bit, 2)) for bit in range(1, bits)
    ]
    pair_load, rest, near_load = loads_of(bits, keep, received)
    pair_load, rest, near_load, held = lax.optimization_barrier((pair_load, rest, near_load, per_head))
    group_b = [
        [swap_chips(rest[bit - 1], mask) for mask in range((2 << bit) - 1, (1 << bit) - 1, -1)] for bit in range(1, bits)
    ]
    pair = swap_chips(pair_load, 1)
    near = swap_cores(near_load)
    half_way = jnp.stack(half_way)
    half_way, held, local_a = lax.optimization_barrier((half_way, held, local_a))
    hop = swap_chips(half_way, 1)
    local_b = local_part(tuple(range(1, heads)), 10**9, table, held, local_a)
    pair, hop, group_b, local_b = lax.optimization_barrier((pair, hop, group_b, local_b))
    pair_o = swap_cores(pair)
    group = jnp.stack([half_way + hop, jnp.stack([sum(pieces) for pieces in group_b])])
    group_o = swap_cores(group)
    wide = own_part(table, per_head, local_b, received, pair, group)
    return last_part(table, per_head, local_b, near, pair_o, group_o, wide)


def solution(mesh):
    part = P(("groups", "seq", "rep"), "head", None)
    return jax.shard_map(
        per_device,
        mesh=mesh,
        in_specs=(part, part, part, part, P(None, "head")),
        out_specs=(part, part, part, part),
        check_vma=False,
    )
```

```python
import functools
import math

import jax
import jax.numpy as jnp
import numpy as np
from jax import lax
from jax.experimental import pallas as pl
from jax.experimental.pallas import tpu as pltpu
from jax.sharding import PartitionSpec as P

BLOCK = 64
TILE = 128
CHUNKS = 2
PARTS = 2
F32 = jnp.float32
BF16 = jnp.bfloat16


def swap_cores(block):
    return lax.ppermute(block, "rep", [(0, 1), (1, 0)])


def swap_chips(block, mask):
    count = lax.axis_size("seq")
    return lax.ppermute(block, "seq", [(chip, chip ^ mask) for chip in range(count)])


def level_scale(level):
    return float(np.float32(1.0) / np.sqrt(np.float32(BLOCK * 2 ** max(level - 1, 0))))


def weight_of(table_ref, head, level):
    return table_ref[pl.ds(head, 1), level : level + 1] * level_scale(level)


def dot_tn(left, right):
    return lax.dot_general(left, right, (((0,), (0,)), ((), ())), preferred_element_type=F32)


def dot_nt(left, right):
    return lax.dot_general(left, right, (((1,), (1,)), ((), ())), preferred_element_type=F32)


def dot_nn(left, right):
    return lax.dot_general(left, right, (((1,), (0,)), ((), ())), preferred_element_type=F32)


def split(value):
    high = value.astype(BF16)
    return high, (value - high.astype(F32)).astype(BF16)


def state_kernel(
    heads, q_ref, k_ref, v_ref, g_ref, levels_ref, send_ref, keep_ref, per_head_ref, table_ref, narrow, wide, arrived, listed
):
    rows = q_ref.shape[0] // heads
    half = heads // 2
    core = lax.axis_index("rep")
    sources = (q_ref, k_ref, v_ref, g_ref)
    length = rows * heads // CHUNKS

    def fetch(which, chunk):
        span = pl.ds(chunk * length, length)
        return pltpu.make_async_copy(sources[which].at[span], narrow.at[which, span], arrived.at[which, chunk])

    pairs = ((1, 2), (0, 3))
    for pair in pairs:
        for chunk in range(CHUNKS):
            for which in pair:
                fetch(which, chunk).start()
    table = pltpu.make_async_copy(levels_ref, table_ref, listed)
    table.start()
    tokens = rows // CHUNKS
    for kind, pair in enumerate(pairs):
        for chunk in range(CHUNKS):
            span, part = pl.ds(chunk * length, length), pl.ds(chunk * tokens, tokens)
            for which in pair:
                fetch(which, chunk).wait()
                wide[which, span] = narrow[which, span].astype(F32)
                for head in range(heads):
                    per_head_ref[which, head, part] = wide[
                        which, pl.ds(chunk * length + head, tokens, stride=heads), :
                    ].astype(BF16)
        for place in range(half):
            for owner, out_ref in ((1 - core, send_ref), (core, keep_ref)):
                head = owner * half + place
                out_ref[kind, place] = dot_tn(per_head_ref[pair[0], head], per_head_ref[pair[1], head])
    table.wait()


def states(flat, table):
    heads = table.shape[0]
    rows, width = flat[0].shape[0] // heads, flat[0].shape[1]
    half = (2, heads // 2, width, width)
    return pl.pallas_call(
        functools.partial(state_kernel, heads),
        out_shape=(
            jax.ShapeDtypeStruct(half, F32),
            jax.ShapeDtypeStruct(half, F32),
            jax.ShapeDtypeStruct((4, heads, rows, width), BF16),
            jax.ShapeDtypeStruct(table.shape, F32),
        ),
        in_specs=[pl.BlockSpec(memory_space=pltpu.HBM)] * 5,
        out_specs=[pl.BlockSpec(memory_space=pltpu.VMEM)] * 4,
        scratch_shapes=[
            pltpu.VMEM((4, rows * heads, width), BF16),
            pltpu.VMEM((4, rows * heads, width), F32),
            pltpu.SemaphoreType.DMA((4, CHUNKS)),
            pltpu.SemaphoreType.DMA,
        ],
        compiler_params=pltpu.CompilerParams(vmem_limit_bytes=24 * 2**20),
        name="states",
    )(*[pltpu.with_memory_space_constraint(array, pltpu.HBM) for array in (*flat, table)])


def local_kernel(chosen, table_ref, per_head_ref, *refs):
    out_ref = refs[-1]
    rows = per_head_ref.shape[2]
    for head in chosen:
        local_head(head, rows, table_ref, per_head_ref.at[:, head], out_ref.at[:, head])


def local_head(head, rows, table_ref, per_head_ref, out_ref):
    tiles = rows // TILE
    inner = (TILE // BLOCK).bit_length()
    weight = [weight_of(table_ref, head, level) for level in range(inner + tiles.bit_length() - 1)]
    row = lax.broadcasted_iota(jnp.int32, (TILE, TILE), 0)
    column = lax.broadcasted_iota(jnp.int32, (TILE, TILE), 1)
    apart = jnp.bitwise_xor(row // BLOCK, column // BLOCK)
    level_mask = jnp.where(apart == 0, weight[0], weight[1])
    for level in range(2, inner):
        level_mask = jnp.where(apart >= 1 << (level - 1), weight[level], level_mask)
    lower = jnp.where(row >= column, level_mask, 0.0)
    upper = jnp.where(row <= column, level_mask, 0.0)
    part = [[per_head_ref[which, pl.ds(tile * TILE, TILE), :] for tile in range(tiles)] for which in range(4)]
    queries, keys, values, out_grad = part

    def sums(states):
        table = {(0, tile): states[tile] for tile in range(tiles)}
        for bit in range(1, tiles.bit_length() - 1):
            for group in range(tiles >> bit):
                table[bit, group] = table[bit - 1, 2 * group] + table[bit - 1, 2 * group + 1]
        return table

    def gather(table, tile, side):
        total = None
        for bit in range(tiles.bit_length() - 1):
            if (tile >> bit) % 2 == side:
                term = weight[inner + bit] * table[bit, (tile >> bit) ^ 1]
                total = term if total is None else total + term
        return [] if total is None else split(total)

    turned = [[block.T for block in array] for array in part]
    q_t, k_t, v_t, g_t = turned
    key_sums = sums([dot_nn(k_t[tile], values[tile]) for tile in range(tiles)])
    key_sums_t = sums([dot_nn(v_t[tile], keys[tile]) for tile in range(tiles)])
    query_sums = sums([dot_nn(q_t[tile], out_grad[tile]) for tile in range(tiles)])
    query_sums_t = sums([dot_nn(g_t[tile], queries[tile]) for tile in range(tiles)])
    held = []
    for tile in range(tiles):
        q, k, v, g = (array[tile] for array in part)
        terms = (
            (dot_nn(q, k_t[tile]) * lower, v, q, gather(key_sums, tile, 1)),
            (dot_nn(g, v_t[tile]) * lower, k, g, gather(key_sums_t, tile, 1)),
            (dot_nn(v, g_t[tile]) * upper, q, v, gather(query_sums_t, tile, 0)),
            (dot_nn(k, q_t[tile]) * upper, g, k, gather(query_sums, tile, 0)),
        )
        held.append(terms)
    for tile in range(tiles):
        for which, (inside, other, mine, pieces) in enumerate(held[tile]):
            result = dot_nn(jnp.concatenate([*split(inside), *([mine, mine] if pieces else [])], 1), jnp.concatenate([other, other, *pieces], 0))
            out_ref[which, pl.ds(tile * TILE, TILE), :] = result


def local_part(chosen, flops, table, per_head, *earlier):
    vmem = pl.BlockSpec(memory_space=pltpu.VMEM)
    return pl.pallas_call(
        functools.partial(local_kernel, chosen),
        out_shape=jax.ShapeDtypeStruct(per_head.shape, F32),
        in_specs=[pl.BlockSpec(memory_space=pltpu.VMEM)] + [vmem] * (1 + len(earlier)),
        out_specs=vmem,
        input_output_aliases={2: 0} if earlier else {},
        compiler_params=pltpu.CompilerParams(vmem_limit_bytes=16 * 2**20),
        cost_estimate=pl.CostEstimate(flops=flops, bytes_accessed=flops // 1000, transcendentals=0),
        name="local",
    )(table, per_head, *earlier)


def far_states(table_ref, head, rows, near, pair, groups):
    core, chip = lax.axis_index("rep"), lax.axis_index("seq")
    terms = [(core == 1, near), (chip % 2 == 1, pair)]
    terms += [((chip >> bit) % 2 == 1, group) for bit, group in enumerate(groups, 1)]
    keys_far = queries_far = 0.0
    for level, (later, piece) in enumerate(terms, (rows // BLOCK).bit_length()):
        weight = weight_of(table_ref, head, level)
        keys_far += jnp.where(later, weight, 0.0) * piece
        queries_far += jnp.where(later, 0.0, weight) * piece
    return [jnp.concatenate(split(state), 0) for state in (keys_far, keys_far.T, queries_far.T, queries_far)]


def far_heads(owner, table_ref, per_head_ref, local_ref, near, pair_ref, group_ref, wide_ref, finish=None, parts=1):
    heads, rows = per_head_ref.shape[1:3]
    half = heads // 2
    chosen = [owner * half + place for place in range(half)]
    states = [
        far_states(table_ref, head, rows, near(place), pair_ref[place], [group_ref[place, bit] for bit in range(group_ref.shape[1])])
        for place, head in enumerate(chosen)
    ]
    part = rows // parts
    for which, source in enumerate((0, 3, 2, 1)):
        for piece in range(parts):
            span = pl.ds(piece * part, part)
            for head, pieces in zip(chosen, states):
                mine = per_head_ref[source, head, span]
                result = local_ref[which, head, span] + dot_nn(jnp.concatenate([mine, mine], 1), pieces[which])
                wide_ref[which, pl.ds(piece * part * heads + head, part, stride=heads), :] = result
            if finish is not None:
                finish(which, pl.ds(piece * part * heads, part * heads))


def own_kernel(table_ref, per_head_ref, local_ref, received_ref, pair_ref, group_ref, wide_ref):
    core = lax.axis_index("rep")
    far_heads(core, table_ref, per_head_ref, local_ref, lambda place: received_ref[1 - core, place],
              pair_ref, group_ref, wide_ref)


def last_kernel(table_ref, per_head_ref, local_ref, near_ref, pair_ref, group_ref, _, *refs):
    out_refs, (wide_ref, narrow, left) = refs[:4], refs[4:]
    copies = []

    def finish(which, span):
        narrow[which, span] = wide_ref[which, span].astype(BF16)
        copy = pltpu.make_async_copy(narrow.at[which, span], out_refs[which].at[span], left.at[len(copies)])
        copy.start()
        copies.append(copy)

    far_heads(1 - lax.axis_index("rep"), table_ref, per_head_ref, local_ref, lambda place: near_ref[place],
              pair_ref, group_ref, wide_ref, finish, PARTS)
    for copy in copies:
        copy.wait()


def own_part(table, per_head, *operands):
    _, heads, rows, width = per_head.shape
    vmem = pl.BlockSpec(memory_space=pltpu.VMEM)
    return pl.pallas_call(
        own_kernel,
        out_shape=jax.ShapeDtypeStruct((4, rows * heads, width), F32),
        in_specs=[pl.BlockSpec(memory_space=pltpu.VMEM)] + [vmem] * (1 + len(operands)),
        out_specs=vmem,
        compiler_params=pltpu.CompilerParams(vmem_limit_bytes=16 * 2**20),
        cost_estimate=pl.CostEstimate(flops=10**9, bytes_accessed=3 * 2**20, transcendentals=0),
        name="own",
    )(table, per_head, *operands)


def last_part(table, per_head, *operands):
    _, heads, rows, width = per_head.shape
    vmem = pl.BlockSpec(memory_space=pltpu.VMEM)
    wide = operands[-1]
    outs = pl.pallas_call(
        last_kernel,
        out_shape=[jax.ShapeDtypeStruct((rows * heads, width), BF16)] * 4 + [jax.ShapeDtypeStruct(wide.shape, F32)],
        in_specs=[pl.BlockSpec(memory_space=pltpu.VMEM)] + [vmem] * (1 + len(operands)),
        out_specs=[pl.BlockSpec(memory_space=pltpu.HBM)] * 4 + [vmem],
        scratch_shapes=[pltpu.VMEM((4, rows * heads, width), BF16), pltpu.SemaphoreType.DMA((4 * PARTS,))],
        input_output_aliases={1 + len(operands): 4},
        compiler_params=pltpu.CompilerParams(vmem_limit_bytes=16 * 2**20),
        name="last",
    )(table, per_head, *operands)
    return tuple(out.reshape(rows, heads, width) for out in outs[:4])


def load_kernel(keep_ref, received_ref, pair_ref, rest_ref, near_ref):
    core, chip = lax.axis_index("rep"), lax.axis_index("seq")
    kind = chip % 2
    pair_ref[...] = keep_ref[kind] + received_ref[kind]
    for bit in range(rest_ref.shape[0]):
        kind = (chip >> (bit + 1)) % 2
        rest_ref[bit] = keep_ref[kind, 1] + received_ref[kind, 1]
    near_ref[...] = keep_ref[core]


def loads_of(bits, keep, received):
    vmem = pl.BlockSpec(memory_space=pltpu.VMEM)
    half, width = keep.shape[1], keep.shape[2]
    shapes = ((half, width, width), (bits - 1, width, width), (half, width, width))
    return pl.pallas_call(
        load_kernel,
        out_shape=[jax.ShapeDtypeStruct(shape, F32) for shape in shapes],
        in_specs=[vmem] * 2,
        out_specs=[vmem] * 3,
        compiler_params=pltpu.CompilerParams(vmem_limit_bytes=4 * 2**20),
        cost_estimate=pl.CostEstimate(flops=10**9, bytes_accessed=3 * 2**20, transcendentals=0),
        name="loads",
    )(keep, received)


def per_device(queries, keys, values, out_grad, level_table):
    rows, heads, width = queries.shape
    half = heads // 2
    bits = lax.axis_size("seq").bit_length() - 1
    chip = lax.axis_index("seq")
    flat = [array.reshape(rows * heads, width) for array in (queries, keys, values, out_grad)]
    send, keep, per_head, table = states(flat, level_table.T)
    received = swap_cores(send)
    local_a = local_part((0,), 10**9, table, per_head)
    received, per_head, local_a = lax.optimization_barrier((received, per_head, local_a))
    first = [
        jnp.where((chip >> bit) % 2 == 1, keep[1, 0] + received[1, 0], keep[0, 0] + received[0, 0])
        for bit in range(1, bits)
    ]
    first, keep, received = lax.optimization_barrier((first, keep, received))
    half_way = [
        sum(swap_chips(first[bit - 1], mask) for mask in range(1 << bit, 2 << bit, 2)) for bit in range(1, bits)
    ]
    pair_load, rest, near_load = loads_of(bits, keep, received)
    pair_load, rest, near_load, held = lax.optimization_barrier((pair_load, rest, near_load, per_head))
    group_b = [
        [swap_chips(rest[bit - 1], mask) for mask in range((2 << bit) - 1, (1 << bit) - 1, -1)] for bit in range(1, bits)
    ]
    pair = swap_chips(pair_load, 1)
    near = swap_cores(near_load)
    half_way = jnp.stack(half_way)
    half_way, held, local_a = lax.optimization_barrier((half_way, held, local_a))
    hop = swap_chips(half_way, 1)
    local_b = local_part(tuple(range(1, heads)), 10**9, table, held, local_a)
    pair, hop, group_b, local_b = lax.optimization_barrier((pair, hop, group_b, local_b))
    pair_o = swap_cores(pair)
    group = jnp.stack([half_way + hop, jnp.stack([sum(pieces) for pieces in group_b])])
    group_o = swap_cores(group)
    wide = own_part(table, per_head, local_b, received, pair, group)
    return last_part(table, per_head, local_b, near, pair_o, group_o, wide)


def solution(mesh):
    part = P(("groups", "seq", "rep"), "head", None)
    return jax.shard_map(
        per_device,
        mesh=mesh,
        in_specs=(part, part, part, part, P(None, "head")),
        out_specs=(part, part, part, part),
        check_vma=False,
    )
```

```python
import functools
import math

import jax
import jax.numpy as jnp
import numpy as np
from jax import lax
from jax.experimental import pallas as pl
from jax.experimental.pallas import tpu as pltpu
from jax.sharding import PartitionSpec as P

BLOCK = 64
TILE = 128
CHUNKS = 2
PARTS = 2
F32 = jnp.float32
BF16 = jnp.bfloat16


def swap_cores(block):
    return lax.ppermute(block, "rep", [(0, 1), (1, 0)])


def swap_chips(block, mask):
    count = lax.axis_size("seq")
    return lax.ppermute(block, "seq", [(chip, chip ^ mask) for chip in range(count)])


def level_scale(level):
    return float(np.float32(1.0) / np.sqrt(np.float32(BLOCK * 2 ** max(level - 1, 0))))


def weight_of(table_ref, head, level):
    return table_ref[pl.ds(head, 1), level : level + 1] * level_scale(level)


def dot_tn(left, right):
    return lax.dot_general(left, right, (((0,), (0,)), ((), ())), preferred_element_type=F32)


def dot_nt(left, right):
    return lax.dot_general(left, right, (((1,), (1,)), ((), ())), preferred_element_type=F32)


def dot_nn(left, right):
    return lax.dot_general(left, right, (((1,), (0,)), ((), ())), preferred_element_type=F32)


def split(value):
    high = value.astype(BF16)
    return high, (value - high.astype(F32)).astype(BF16)


def state_kernel(
    heads, q_ref, k_ref, v_ref, g_ref, levels_ref, send_a_ref, send_b_ref, keep_ref, per_head_ref, table_ref, narrow, wide, arrived, listed
):
    rows = q_ref.shape[0] // heads
    half = heads // 2
    core = lax.axis_index("rep")
    sources = (q_ref, k_ref, v_ref, g_ref)
    length = rows * heads // CHUNKS

    def fetch(which, chunk):
        span = pl.ds(chunk * length, length)
        return pltpu.make_async_copy(sources[which].at[span], narrow.at[which, span], arrived.at[which, chunk])

    pairs = ((1, 2), (0, 3))
    for pair in pairs:
        for chunk in range(CHUNKS):
            for which in pair:
                fetch(which, chunk).start()
    table = pltpu.make_async_copy(levels_ref, table_ref, listed)
    table.start()
    tokens = rows // CHUNKS
    for kind, pair in enumerate(pairs):
        for chunk in range(CHUNKS):
            span, part = pl.ds(chunk * length, length), pl.ds(chunk * tokens, tokens)
            for which in pair:
                fetch(which, chunk).wait()
                wide[which, span] = narrow[which, span].astype(F32)
                for head in range(heads):
                    per_head_ref[which, head, part] = wide[
                        which, pl.ds(chunk * length + head, tokens, stride=heads), :
                    ].astype(BF16)
        for place in range(half):
            for sent in (True, False):
                head = (1 - core if sent else core) * half + place
                state = dot_tn(per_head_ref[pair[0], head], per_head_ref[pair[1], head])
                if not sent:
                    keep_ref[kind, place] = state
                elif place == 0:
                    send_a_ref[kind] = state
                else:
                    send_b_ref[kind, place - 1] = state
    table.wait()


def states(flat, table):
    heads = table.shape[0]
    rows, width = flat[0].shape[0] // heads, flat[0].shape[1]
    half = (2, heads // 2, width, width)
    return pl.pallas_call(
        functools.partial(state_kernel, heads),
        out_shape=(
            jax.ShapeDtypeStruct((2, width, width), F32),
            jax.ShapeDtypeStruct((2, heads // 2 - 1, width, width), F32),
            jax.ShapeDtypeStruct(half, F32),
            jax.ShapeDtypeStruct((4, heads, rows, width), BF16),
            jax.ShapeDtypeStruct(table.shape, F32),
        ),
        in_specs=[pl.BlockSpec(memory_space=pltpu.HBM)] * 5,
        out_specs=[pl.BlockSpec(memory_space=pltpu.VMEM)] * 5,
        scratch_shapes=[
            pltpu.VMEM((4, rows * heads, width), BF16),
            pltpu.VMEM((4, rows * heads, width), F32),
            pltpu.SemaphoreType.DMA((4, CHUNKS)),
            pltpu.SemaphoreType.DMA,
        ],
        compiler_params=pltpu.CompilerParams(vmem_limit_bytes=24 * 2**20),
        name="states",
    )(*[pltpu.with_memory_space_constraint(array, pltpu.HBM) for array in (*flat, table)])


def local_kernel(chosen, table_ref, per_head_ref, *refs):
    out_ref = refs[-1]
    rows = per_head_ref.shape[2]
    for head, sides in chosen:
        local_head(head, sides, rows, table_ref, per_head_ref.at[:, head], out_ref.at[:, head])


def local_head(head, sides, rows, table_ref, per_head_ref, out_ref):
    tiles = rows // TILE
    inner = (TILE // BLOCK).bit_length()
    weight = [weight_of(table_ref, head, level) for level in range(inner + tiles.bit_length() - 1)]
    row = lax.broadcasted_iota(jnp.int32, (TILE, TILE), 0)
    column = lax.broadcasted_iota(jnp.int32, (TILE, TILE), 1)
    apart = jnp.bitwise_xor(row // BLOCK, column // BLOCK)
    level_mask = jnp.where(apart == 0, weight[0], weight[1])
    for level in range(2, inner):
        level_mask = jnp.where(apart >= 1 << (level - 1), weight[level], level_mask)
    lower = jnp.where(row >= column, level_mask, 0.0)
    upper = jnp.where(row <= column, level_mask, 0.0)
    part = [[per_head_ref[which, pl.ds(tile * TILE, TILE), :] for tile in range(tiles)] for which in range(4)]
    queries, keys, values, out_grad = part

    def sums(states):
        table = {(0, tile): states[tile] for tile in range(tiles)}
        for bit in range(1, tiles.bit_length() - 1):
            for group in range(tiles >> bit):
                table[bit, group] = table[bit - 1, 2 * group] + table[bit - 1, 2 * group + 1]
        return table

    def gather(table, tile, side):
        total = None
        for bit in range(tiles.bit_length() - 1):
            if (tile >> bit) % 2 == side:
                term = weight[inner + bit] * table[bit, (tile >> bit) ^ 1]
                total = term if total is None else total + term
        return [] if total is None else split(total)

    turned = [[block.T for block in array] for array in part]
    q_t, k_t, v_t, g_t = turned
    if 0 in sides:
        key_sums = sums([dot_nn(k_t[tile], values[tile]) for tile in range(tiles)])
        key_sums_t = sums([dot_nn(v_t[tile], keys[tile]) for tile in range(tiles)])
    if 1 in sides:
        query_sums = sums([dot_nn(q_t[tile], out_grad[tile]) for tile in range(tiles)])
        query_sums_t = sums([dot_nn(g_t[tile], queries[tile]) for tile in range(tiles)])
    held = []
    for tile in range(tiles):
        q, k, v, g = (array[tile] for array in part)
        terms = []
        if 0 in sides:
            terms += [
                (0, dot_nn(q, k_t[tile]) * lower, v, q, gather(key_sums, tile, 1)),
                (1, dot_nn(g, v_t[tile]) * lower, k, g, gather(key_sums_t, tile, 1)),
            ]
        if 1 in sides:
            terms += [
                (2, dot_nn(v, g_t[tile]) * upper, q, v, gather(query_sums_t, tile, 0)),
                (3, dot_nn(k, q_t[tile]) * upper, g, k, gather(query_sums, tile, 0)),
            ]
        held.append(terms)
    for tile in range(tiles):
        for which, inside, other, mine, pieces in held[tile]:
            result = dot_nn(jnp.concatenate([*split(inside), *([mine, mine] if pieces else [])], 1), jnp.concatenate([other, other, *pieces], 0))
            out_ref[which, pl.ds(tile * TILE, TILE), :] = result


def local_part(chosen, flops, table, per_head, *earlier):
    vmem = pl.BlockSpec(memory_space=pltpu.VMEM)
    return pl.pallas_call(
        functools.partial(local_kernel, chosen),
        out_shape=jax.ShapeDtypeStruct(per_head.shape, F32),
        in_specs=[pl.BlockSpec(memory_space=pltpu.VMEM)] + [vmem] * (1 + len(earlier)),
        out_specs=vmem,
        input_output_aliases={2: 0} if earlier else {},
        compiler_params=pltpu.CompilerParams(vmem_limit_bytes=16 * 2**20),
        cost_estimate=pl.CostEstimate(flops=flops, bytes_accessed=flops // 1000, transcendentals=0),
        name="local",
    )(table, per_head, *earlier)


def far_states(table_ref, head, rows, near, pair, groups):
    core, chip = lax.axis_index("rep"), lax.axis_index("seq")
    terms = [(core == 1, near), (chip % 2 == 1, pair)]
    terms += [((chip >> bit) % 2 == 1, group) for bit, group in enumerate(groups, 1)]
    keys_far = queries_far = 0.0
    for level, (later, piece) in enumerate(terms, (rows // BLOCK).bit_length()):
        weight = weight_of(table_ref, head, level)
        keys_far += jnp.where(later, weight, 0.0) * piece
        queries_far += jnp.where(later, 0.0, weight) * piece
    return [jnp.concatenate(split(state), 0) for state in (keys_far, keys_far.T, queries_far.T, queries_far)]


def far_heads(owner, table_ref, per_head_ref, local_ref, near, pair_ref, group_ref, wide_ref, finish=None, parts=1):
    heads, rows = per_head_ref.shape[1:3]
    half = heads // 2
    chosen = [owner * half + place for place in range(half)]
    states = [
        far_states(table_ref, head, rows, near(place), pair_ref[place], [group_ref[place, bit] for bit in range(group_ref.shape[1])])
        for place, head in enumerate(chosen)
    ]
    part = rows // parts
    for which, source in enumerate((0, 3, 2, 1)):
        for piece in range(parts):
            span = pl.ds(piece * part, part)
            for head, pieces in zip(chosen, states):
                mine = per_head_ref[source, head, span]
                result = local_ref[which, head, span] + dot_nn(jnp.concatenate([mine, mine], 1), pieces[which])
                wide_ref[which, pl.ds(piece * part * heads + head, part, stride=heads), :] = result
            if finish is not None:
                finish(which, pl.ds(piece * part * heads, part * heads))


def own_kernel(table_ref, per_head_ref, local_ref, received_a_ref, received_b_ref, pair_ref, group_ref, wide_ref):
    core = lax.axis_index("rep")
    far_heads(core, table_ref, per_head_ref, local_ref, lambda place: received_b_ref[1 - core, place - 1] if place else received_a_ref[1 - core],
              pair_ref, group_ref, wide_ref)


def last_kernel(table_ref, per_head_ref, local_ref, near_ref, pair_ref, group_ref, _, *refs):
    out_refs, (wide_ref, narrow, left) = refs[:4], refs[4:]
    copies = []

    def finish(which, span):
        narrow[which, span] = wide_ref[which, span].astype(BF16)
        copy = pltpu.make_async_copy(narrow.at[which, span], out_refs[which].at[span], left.at[len(copies)])
        copy.start()
        copies.append(copy)

    far_heads(1 - lax.axis_index("rep"), table_ref, per_head_ref, local_ref, lambda place: near_ref[place],
              pair_ref, group_ref, wide_ref, finish, PARTS)
    for copy in copies:
        copy.wait()


def own_part(table, per_head, *operands):
    _, heads, rows, width = per_head.shape
    vmem = pl.BlockSpec(memory_space=pltpu.VMEM)
    return pl.pallas_call(
        own_kernel,
        out_shape=jax.ShapeDtypeStruct((4, rows * heads, width), F32),
        in_specs=[pl.BlockSpec(memory_space=pltpu.VMEM)] + [vmem] * (1 + len(operands)),
        out_specs=vmem,
        compiler_params=pltpu.CompilerParams(vmem_limit_bytes=16 * 2**20),
        cost_estimate=pl.CostEstimate(flops=10**9, bytes_accessed=3 * 2**20, transcendentals=0),
        name="own",
    )(table, per_head, *operands)


def last_part(table, per_head, *operands):
    _, heads, rows, width = per_head.shape
    vmem = pl.BlockSpec(memory_space=pltpu.VMEM)
    wide = operands[-1]
    outs = pl.pallas_call(
        last_kernel,
        out_shape=[jax.ShapeDtypeStruct((rows * heads, width), BF16)] * 4 + [jax.ShapeDtypeStruct(wide.shape, F32)],
        in_specs=[pl.BlockSpec(memory_space=pltpu.VMEM)] + [vmem] * (1 + len(operands)),
        out_specs=[pl.BlockSpec(memory_space=pltpu.HBM)] * 4 + [vmem],
        scratch_shapes=[pltpu.VMEM((4, rows * heads, width), BF16), pltpu.SemaphoreType.DMA((4 * PARTS,))],
        input_output_aliases={1 + len(operands): 4},
        compiler_params=pltpu.CompilerParams(vmem_limit_bytes=16 * 2**20),
        name="last",
    )(table, per_head, *operands)
    return tuple(out.reshape(rows, heads, width) for out in outs[:4])


def load_kernel(keep_ref, received_a_ref, received_b_ref, pair_ref, rest_ref, near_ref):
    core, chip = lax.axis_index("rep"), lax.axis_index("seq")
    kind = chip % 2
    pair_ref[0] = keep_ref[kind, 0] + received_a_ref[kind]
    pair_ref[1:] = keep_ref[kind, 1:] + received_b_ref[kind]
    for bit in range(rest_ref.shape[0]):
        kind = (chip >> (bit + 1)) % 2
        rest_ref[bit] = keep_ref[kind, 1] + received_b_ref[kind, 0]
    near_ref[...] = keep_ref[core]


def loads_of(bits, keep, *received):
    vmem = pl.BlockSpec(memory_space=pltpu.VMEM)
    half, width = keep.shape[1], keep.shape[2]
    shapes = ((half, width, width), (bits - 1, width, width), (half, width, width))
    return pl.pallas_call(
        load_kernel,
        out_shape=[jax.ShapeDtypeStruct(shape, F32) for shape in shapes],
        in_specs=[vmem] * 3,
        out_specs=[vmem] * 3,
        compiler_params=pltpu.CompilerParams(vmem_limit_bytes=4 * 2**20),
        cost_estimate=pl.CostEstimate(flops=10**9, bytes_accessed=3 * 2**20, transcendentals=0),
        name="loads",
    )(keep, *received)


def per_device(queries, keys, values, out_grad, level_table):
    rows, heads, width = queries.shape
    half = heads // 2
    bits = lax.axis_size("seq").bit_length() - 1
    chip = lax.axis_index("seq")
    flat = [array.reshape(rows * heads, width) for array in (queries, keys, values, out_grad)]
    send_a, send_b, keep, per_head, table = states(flat, level_table.T)
    received_a, received_b = swap_cores(send_a), swap_cores(send_b)
    local_a = local_part([(0, (0,))], 10**9, table, per_head)
    received_a, per_head, local_a = lax.optimization_barrier((received_a, per_head, local_a))
    first = [
        jnp.where((chip >> bit) % 2 == 1, keep[1, 0] + received_a[1], keep[0, 0] + received_a[0])
        for bit in range(1, bits)
    ]
    first, keep, received_a = lax.optimization_barrier((first, keep, received_a))
    half_way = [
        sum(swap_chips(first[bit - 1], mask) for mask in range(1 << bit, 2 << bit, 2)) for bit in range(1, bits)
    ]
    pair_load, rest, near_load = loads_of(bits, keep, received_a, received_b)
    pair_load, rest, near_load, held = lax.optimization_barrier((pair_load, rest, near_load, per_head))
    group_b = [
        [swap_chips(rest[bit - 1], mask) for mask in range((2 << bit) - 1, (1 << bit) - 1, -1)] for bit in range(1, bits)
    ]
    pair = swap_chips(pair_load, 1)
    near = swap_cores(near_load)
    half_way = jnp.stack(half_way)
    half_way, held, local_a = lax.optimization_barrier((half_way, held, local_a))
    hop = swap_chips(half_way, 1)
    local_b = local_part([(0, (1,))] + [(head, (0, 1)) for head in range(1, heads)], 10**9, table, held, local_a)
    pair, hop, group_b, local_b = lax.optimization_barrier((pair, hop, group_b, local_b))
    pair_o = swap_cores(pair)
    group = jnp.stack([half_way + hop, jnp.stack([sum(pieces) for pieces in group_b])])
    group_o = swap_cores(group)
    wide = own_part(table, per_head, local_b, received_a, received_b, pair, group)
    return last_part(table, per_head, local_b, near, pair_o, group_o, wide)


def solution(mesh):
    part = P(("groups", "seq", "rep"), "head", None)
    return jax.shard_map(
        per_device,
        mesh=mesh,
        in_specs=(part, part, part, part, P(None, "head")),
        out_specs=(part, part, part, part),
        check_vma=False,
    )
```

```python
import functools
import math

import jax
import jax.numpy as jnp
import numpy as np
from jax import lax
from jax.experimental import pallas as pl
from jax.experimental.pallas import tpu as pltpu
from jax.sharding import PartitionSpec as P

BLOCK = 64
TILE = 128
CHUNKS = 2
PARTS = 2
FIRST = 160
F32 = jnp.float32
BF16 = jnp.bfloat16


def swap_cores(block):
    return lax.ppermute(block, "rep", [(0, 1), (1, 0)])


def swap_chips(block, mask):
    count = lax.axis_size("seq")
    return lax.ppermute(block, "seq", [(chip, chip ^ mask) for chip in range(count)])


def level_scale(level):
    return float(np.float32(1.0) / np.sqrt(np.float32(BLOCK * 2 ** max(level - 1, 0))))


def weight_of(table_ref, head, level):
    return table_ref[pl.ds(head, 1), level : level + 1] * level_scale(level)


def dot_tn(left, right):
    return lax.dot_general(left, right, (((0,), (0,)), ((), ())), preferred_element_type=F32)


def dot_nt(left, right):
    return lax.dot_general(left, right, (((1,), (1,)), ((), ())), preferred_element_type=F32)


def dot_nn(left, right):
    return lax.dot_general(left, right, (((1,), (0,)), ((), ())), preferred_element_type=F32)


def split(value):
    high = value.astype(BF16)
    return high, (value - high.astype(F32)).astype(BF16)


def state_kernel(
    heads, q_ref, k_ref, v_ref, g_ref, levels_ref, send_a_ref, send_b_ref, keep_ref, per_head_ref, table_ref, narrow, wide, arrived, listed
):
    rows = q_ref.shape[0] // heads
    half = heads // 2
    core = lax.axis_index("rep")
    sources = (q_ref, k_ref, v_ref, g_ref)
    length = rows * heads // CHUNKS

    def fetch(which, chunk):
        span = pl.ds(chunk * length, length)
        return pltpu.make_async_copy(sources[which].at[span], narrow.at[which, span], arrived.at[which, chunk])

    pairs = ((1, 2), (0, 3))
    for pair in pairs:
        for chunk in range(CHUNKS):
            for which in pair:
                fetch(which, chunk).start()
    table = pltpu.make_async_copy(levels_ref, table_ref, listed)
    table.start()
    tokens = rows // CHUNKS
    for kind, pair in enumerate(pairs):
        for chunk in range(CHUNKS):
            span, part = pl.ds(chunk * length, length), pl.ds(chunk * tokens, tokens)
            for which in pair:
                fetch(which, chunk).wait()
                wide[which, span] = narrow[which, span].astype(F32)
                for head in range(heads):
                    per_head_ref[which, head, part] = wide[
                        which, pl.ds(chunk * length + head, tokens, stride=heads), :
                    ].astype(BF16)
        for place in range(half):
            for sent in (True, False):
                head = (1 - core if sent else core) * half + place
                state = dot_tn(per_head_ref[pair[0], head], per_head_ref[pair[1], head])
                low, high = place * state.shape[0], (place + 1) * state.shape[0]
                if not sent:
                    keep_ref[kind, low:high] = state
                    continue
                cut = min(max(send_a_ref.shape[1], low), high)
                if cut > low:
                    send_a_ref[kind, low:cut] = state[: cut - low]
                if cut < high:
                    start = cut - send_a_ref.shape[1]
                    send_b_ref[kind, start : start + high - cut] = state[cut - low :]
    table.wait()


def states(flat, table):
    heads = table.shape[0]
    rows, width = flat[0].shape[0] // heads, flat[0].shape[1]
    tall = heads // 2 * width
    first = FIRST * width // 128
    return pl.pallas_call(
        functools.partial(state_kernel, heads),
        out_shape=(
            jax.ShapeDtypeStruct((2, first, width), F32),
            jax.ShapeDtypeStruct((2, tall - first, width), F32),
            jax.ShapeDtypeStruct((2, tall, width), F32),
            jax.ShapeDtypeStruct((4, heads, rows, width), BF16),
            jax.ShapeDtypeStruct(table.shape, F32),
        ),
        in_specs=[pl.BlockSpec(memory_space=pltpu.HBM)] * 5,
        out_specs=[pl.BlockSpec(memory_space=pltpu.VMEM)] * 5,
        scratch_shapes=[
            pltpu.VMEM((4, rows * heads, width), BF16),
            pltpu.VMEM((4, rows * heads, width), F32),
            pltpu.SemaphoreType.DMA((4, CHUNKS)),
            pltpu.SemaphoreType.DMA,
        ],
        compiler_params=pltpu.CompilerParams(vmem_limit_bytes=24 * 2**20),
        name="states",
    )(*[pltpu.with_memory_space_constraint(array, pltpu.HBM) for array in (*flat, table)])


def local_kernel(chosen, table_ref, per_head_ref, *refs):
    out_ref = refs[-1]
    rows = per_head_ref.shape[2]
    for head, sides in chosen:
        local_head(head, sides, rows, table_ref, per_head_ref.at[:, head], out_ref.at[:, head])


def local_head(head, sides, rows, table_ref, per_head_ref, out_ref):
    tiles = rows // TILE
    inner = (TILE // BLOCK).bit_length()
    weight = [weight_of(table_ref, head, level) for level in range(inner + tiles.bit_length() - 1)]
    row = lax.broadcasted_iota(jnp.int32, (TILE, TILE), 0)
    column = lax.broadcasted_iota(jnp.int32, (TILE, TILE), 1)
    apart = jnp.bitwise_xor(row // BLOCK, column // BLOCK)
    level_mask = jnp.where(apart == 0, weight[0], weight[1])
    for level in range(2, inner):
        level_mask = jnp.where(apart >= 1 << (level - 1), weight[level], level_mask)
    lower = jnp.where(row >= column, level_mask, 0.0)
    upper = jnp.where(row <= column, level_mask, 0.0)
    part = [[per_head_ref[which, pl.ds(tile * TILE, TILE), :] for tile in range(tiles)] for which in range(4)]
    queries, keys, values, out_grad = part

    def sums(states):
        table = {(0, tile): states[tile] for tile in range(tiles)}
        for bit in range(1, tiles.bit_length() - 1):
            for group in range(tiles >> bit):
                table[bit, group] = table[bit - 1, 2 * group] + table[bit - 1, 2 * group + 1]
        return table

    def gather(table, tile, side):
        total = None
        for bit in range(tiles.bit_length() - 1):
            if (tile >> bit) % 2 == side:
                term = weight[inner + bit] * table[bit, (tile >> bit) ^ 1]
                total = term if total is None else total + term
        return [] if total is None else split(total)

    turned = [[block.T for block in array] for array in part]
    q_t, k_t, v_t, g_t = turned
    if 0 in sides:
        key_sums = sums([dot_nn(k_t[tile], values[tile]) for tile in range(tiles)])
        key_sums_t = sums([dot_nn(v_t[tile], keys[tile]) for tile in range(tiles)])
    if 1 in sides:
        query_sums = sums([dot_nn(q_t[tile], out_grad[tile]) for tile in range(tiles)])
        query_sums_t = sums([dot_nn(g_t[tile], queries[tile]) for tile in range(tiles)])
    held = []
    for tile in range(tiles):
        q, k, v, g = (array[tile] for array in part)
        terms = []
        if 0 in sides:
            terms += [
                (0, dot_nn(q, k_t[tile]) * lower, v, q, gather(key_sums, tile, 1)),
                (1, dot_nn(g, v_t[tile]) * lower, k, g, gather(key_sums_t, tile, 1)),
            ]
        if 1 in sides:
            terms += [
                (2, dot_nn(v, g_t[tile]) * upper, q, v, gather(query_sums_t, tile, 0)),
                (3, dot_nn(k, q_t[tile]) * upper, g, k, gather(query_sums, tile, 0)),
            ]
        held.append(terms)
    for tile in range(tiles):
        for which, inside, other, mine, pieces in held[tile]:
            result = dot_nn(jnp.concatenate([*split(inside), *([mine, mine] if pieces else [])], 1), jnp.concatenate([other, other, *pieces], 0))
            out_ref[which, pl.ds(tile * TILE, TILE), :] = result


def local_part(chosen, flops, table, per_head, *earlier):
    vmem = pl.BlockSpec(memory_space=pltpu.VMEM)
    return pl.pallas_call(
        functools.partial(local_kernel, chosen),
        out_shape=jax.ShapeDtypeStruct(per_head.shape, F32),
        in_specs=[pl.BlockSpec(memory_space=pltpu.VMEM)] + [vmem] * (1 + len(earlier)),
        out_specs=vmem,
        input_output_aliases={2: 0} if earlier else {},
        compiler_params=pltpu.CompilerParams(vmem_limit_bytes=16 * 2**20),
        cost_estimate=pl.CostEstimate(flops=flops, bytes_accessed=flops // 1000, transcendentals=0),
        name="local",
    )(table, per_head, *earlier)


def far_states(table_ref, head, rows, near, pair, groups):
    core, chip = lax.axis_index("rep"), lax.axis_index("seq")
    terms = [(core == 1, near), (chip % 2 == 1, pair)]
    terms += [((chip >> bit) % 2 == 1, group) for bit, group in enumerate(groups, 1)]
    keys_far = queries_far = 0.0
    for level, (later, piece) in enumerate(terms, (rows // BLOCK).bit_length()):
        weight = weight_of(table_ref, head, level)
        keys_far += jnp.where(later, weight, 0.0) * piece
        queries_far += jnp.where(later, 0.0, weight) * piece
    return [jnp.concatenate(split(state), 0) for state in (keys_far, keys_far.T, queries_far.T, queries_far)]


def far_heads(owner, table_ref, per_head_ref, local_ref, near, pair_ref, group_ref, wide_ref, finish=None, parts=1):
    heads, rows = per_head_ref.shape[1:3]
    half = heads // 2
    chosen = [owner * half + place for place in range(half)]
    width = pair_ref.shape[1]
    spans = [slice(place * width, (place + 1) * width) for place in range(half)]
    states = [
        far_states(table_ref, head, rows, near(span), pair_ref[span], [group_ref[bit, span] for bit in range(group_ref.shape[0])])
        for head, span in zip(chosen, spans)
    ]
    part = rows // parts
    for which, source in enumerate((0, 3, 2, 1)):
        for piece in range(parts):
            span = pl.ds(piece * part, part)
            for head, pieces in zip(chosen, states):
                mine = per_head_ref[source, head, span]
                result = local_ref[which, head, span] + dot_nn(jnp.concatenate([mine, mine], 1), pieces[which])
                wide_ref[which, pl.ds(piece * part * heads + head, part, stride=heads), :] = result
            if finish is not None:
                finish(which, pl.ds(piece * part * heads, part * heads))


def own_kernel(table_ref, per_head_ref, local_ref, received_a_ref, received_b_ref, pair_ref, group_ref, wide_ref):
    core = lax.axis_index("rep")
    far_heads(core, table_ref, per_head_ref, local_ref, lambda span: jnp.concatenate([received_a_ref[1 - core], received_b_ref[1 - core]], 0)[span],
              pair_ref, group_ref, wide_ref)


def last_kernel(table_ref, per_head_ref, local_ref, near_ref, pair_ref, group_ref, _, *refs):
    out_refs, (wide_ref, narrow, left) = refs[:4], refs[4:]
    copies = []

    def finish(which, span):
        narrow[which, span] = wide_ref[which, span].astype(BF16)
        copy = pltpu.make_async_copy(narrow.at[which, span], out_refs[which].at[span], left.at[len(copies)])
        copy.start()
        copies.append(copy)

    far_heads(1 - lax.axis_index("rep"), table_ref, per_head_ref, local_ref, lambda span: near_ref[span],
              pair_ref, group_ref, wide_ref, finish, PARTS)
    for copy in copies:
        copy.wait()


def own_part(table, per_head, *operands):
    _, heads, rows, width = per_head.shape
    vmem = pl.BlockSpec(memory_space=pltpu.VMEM)
    return pl.pallas_call(
        own_kernel,
        out_shape=jax.ShapeDtypeStruct((4, rows * heads, width), F32),
        in_specs=[pl.BlockSpec(memory_space=pltpu.VMEM)] + [vmem] * (1 + len(operands)),
        out_specs=vmem,
        compiler_params=pltpu.CompilerParams(vmem_limit_bytes=16 * 2**20),
        cost_estimate=pl.CostEstimate(flops=10**9, bytes_accessed=3 * 2**20, transcendentals=0),
        name="own",
    )(table, per_head, *operands)


def last_part(table, per_head, *operands):
    _, heads, rows, width = per_head.shape
    vmem = pl.BlockSpec(memory_space=pltpu.VMEM)
    wide = operands[-1]
    outs = pl.pallas_call(
        last_kernel,
        out_shape=[jax.ShapeDtypeStruct((rows * heads, width), BF16)] * 4 + [jax.ShapeDtypeStruct(wide.shape, F32)],
        in_specs=[pl.BlockSpec(memory_space=pltpu.VMEM)] + [vmem] * (1 + len(operands)),
        out_specs=[pl.BlockSpec(memory_space=pltpu.HBM)] * 4 + [vmem],
        scratch_shapes=[pltpu.VMEM((4, rows * heads, width), BF16), pltpu.SemaphoreType.DMA((4 * PARTS,))],
        input_output_aliases={1 + len(operands): 4},
        compiler_params=pltpu.CompilerParams(vmem_limit_bytes=16 * 2**20),
        name="last",
    )(table, per_head, *operands)
    return tuple(out.reshape(rows, heads, width) for out in outs[:4])


def load_kernel(keep_ref, received_a_ref, received_b_ref, pair_ref, rest_ref, near_ref):
    core, chip = lax.axis_index("rep"), lax.axis_index("seq")
    first = received_a_ref.shape[1]
    kind = chip % 2
    pair_ref[:first] = keep_ref[kind, :first] + received_a_ref[kind]
    pair_ref[first:] = keep_ref[kind, first:] + received_b_ref[kind]
    for bit in range(rest_ref.shape[0]):
        kind = (chip >> (bit + 1)) % 2
        rest_ref[bit] = keep_ref[kind, first:] + received_b_ref[kind]
    near_ref[...] = keep_ref[core]


def loads_of(bits, keep, *received):
    vmem = pl.BlockSpec(memory_space=pltpu.VMEM)
    tall, width = keep.shape[1:]
    shapes = ((tall, width), (bits - 1, received[1].shape[1], width), (tall, width))
    return pl.pallas_call(
        load_kernel,
        out_shape=[jax.ShapeDtypeStruct(shape, F32) for shape in shapes],
        in_specs=[vmem] * 3,
        out_specs=[vmem] * 3,
        compiler_params=pltpu.CompilerParams(vmem_limit_bytes=4 * 2**20),
        cost_estimate=pl.CostEstimate(flops=10**9, bytes_accessed=3 * 2**20, transcendentals=0),
        name="loads",
    )(keep, *received)


def per_device(queries, keys, values, out_grad, level_table):
    rows, heads, width = queries.shape
    half = heads // 2
    bits = lax.axis_size("seq").bit_length() - 1
    chip = lax.axis_index("seq")
    flat = [array.reshape(rows * heads, width) for array in (queries, keys, values, out_grad)]
    send_a, send_b, keep, per_head, table = states(flat, level_table.T)
    received_a, received_b = swap_cores(send_a), swap_cores(send_b)
    local_a = local_part([(0, (0,))], 10**9, table, per_head)
    received_a, per_head, local_a = lax.optimization_barrier((received_a, per_head, local_a))
    first_rows = received_a.shape[1]
    first = [
        jnp.where((chip >> bit) % 2 == 1, keep[1, :first_rows] + received_a[1], keep[0, :first_rows] + received_a[0])
        for bit in range(1, bits)
    ]
    first, keep, received_a = lax.optimization_barrier((first, keep, received_a))
    half_way = [
        sum(swap_chips(first[bit - 1], mask) for mask in range(1 << bit, 2 << bit, 2)) for bit in range(1, bits)
    ]
    pair_load, rest, near_load = loads_of(bits, keep, received_a, received_b)
    pair_load, rest, near_load, held = lax.optimization_barrier((pair_load, rest, near_load, per_head))
    group_b = [
        [swap_chips(rest[bit - 1], mask) for mask in range((2 << bit) - 1, (1 << bit) - 1, -1)] for bit in range(1, bits)
    ]
    pair = swap_chips(pair_load, 1)
    near = swap_cores(near_load)
    half_way = jnp.stack(half_way)
    half_way, held, local_a = lax.optimization_barrier((half_way, held, local_a))
    hop = swap_chips(half_way, 1)
    local_b = local_part([(0, (1,))] + [(head, (0, 1)) for head in range(1, heads)], 10**9, table, held, local_a)
    pair, hop, group_b, local_b = lax.optimization_barrier((pair, hop, group_b, local_b))
    pair_o = swap_cores(pair)
    group = jnp.concatenate([half_way + hop, jnp.stack([sum(pieces) for pieces in group_b])], 1)
    group_o = swap_cores(group)
    wide = own_part(table, per_head, local_b, received_a, received_b, pair, group)
    return last_part(table, per_head, local_b, near, pair_o, group_o, wide)


def solution(mesh):
    part = P(("groups", "seq", "rep"), "head", None)
    return jax.shard_map(
        per_device,
        mesh=mesh,
        in_specs=(part, part, part, part, P(None, "head")),
        out_specs=(part, part, part, part),
        check_vma=False,
    )
```

```python
import functools
import math

import jax
import jax.numpy as jnp
import numpy as np
from jax import lax
from jax.experimental import pallas as pl
from jax.experimental.pallas import tpu as pltpu
from jax.sharding import PartitionSpec as P

BLOCK = 64
TILE = 128
CHUNKS = 2
PARTS = 2
FIRST = 160
F32 = jnp.float32
BF16 = jnp.bfloat16


def swap_cores(block):
    return lax.ppermute(block, "rep", [(0, 1), (1, 0)])


def swap_chips(block, mask):
    count = lax.axis_size("seq")
    return lax.ppermute(block, "seq", [(chip, chip ^ mask) for chip in range(count)])


def level_scale(level):
    return float(np.float32(1.0) / np.sqrt(np.float32(BLOCK * 2 ** max(level - 1, 0))))


def weight_of(table_ref, head, level):
    return table_ref[pl.ds(head, 1), level : level + 1] * level_scale(level)


def dot_tn(left, right):
    return lax.dot_general(left, right, (((0,), (0,)), ((), ())), preferred_element_type=F32)


def dot_nt(left, right):
    return lax.dot_general(left, right, (((1,), (1,)), ((), ())), preferred_element_type=F32)


def dot_nn(left, right):
    return lax.dot_general(left, right, (((1,), (0,)), ((), ())), preferred_element_type=F32)


def split(value):
    high = value.astype(BF16)
    return high, (value - high.astype(F32)).astype(BF16)


def state_kernel(
    heads, q_ref, k_ref, v_ref, g_ref, levels_ref, send_a_ref, send_b_ref, keep_ref, per_head_ref, table_ref, narrow, wide, arrived, listed
):
    rows = q_ref.shape[0] // heads
    half = heads // 2
    core = lax.axis_index("rep")
    sources = (q_ref, k_ref, v_ref, g_ref)
    length = rows * heads // CHUNKS

    def fetch(which, chunk):
        span = pl.ds(chunk * length, length)
        return pltpu.make_async_copy(sources[which].at[span], narrow.at[which, span], arrived.at[which, chunk])

    pairs = ((1, 2), (0, 3))
    for pair in pairs:
        for chunk in range(CHUNKS):
            for which in pair:
                fetch(which, chunk).start()
    table = pltpu.make_async_copy(levels_ref, table_ref, listed)
    table.start()
    tokens = rows // CHUNKS
    for kind, pair in enumerate(pairs):
        for chunk in range(CHUNKS):
            span, part = pl.ds(chunk * length, length), pl.ds(chunk * tokens, tokens)
            for which in pair:
                fetch(which, chunk).wait()
                wide[which, span] = narrow[which, span].astype(F32)
                for head in range(heads):
                    per_head_ref[which, head, part] = wide[
                        which, pl.ds(chunk * length + head, tokens, stride=heads), :
                    ].astype(BF16)
        for place in range(half):
            for sent in (True, False):
                head = (1 - core if sent else core) * half + place
                state = dot_tn(per_head_ref[pair[0], head], per_head_ref[pair[1], head])
                low, high = place * state.shape[0], (place + 1) * state.shape[0]
                if not sent:
                    keep_ref[kind, low:high] = state
                    continue
                cut = min(max(send_a_ref.shape[1], low), high)
                if cut > low:
                    send_a_ref[kind, low:cut] = state[: cut - low]
                if cut < high:
                    start = cut - send_a_ref.shape[1]
                    send_b_ref[kind, start : start + high - cut] = state[cut - low :]
    table.wait()


def states(flat, table):
    heads = table.shape[0]
    rows, width = flat[0].shape[0] // heads, flat[0].shape[1]
    tall = heads // 2 * width
    first = FIRST * width // 128
    return pl.pallas_call(
        functools.partial(state_kernel, heads),
        out_shape=(
            jax.ShapeDtypeStruct((2, first, width), F32),
            jax.ShapeDtypeStruct((2, tall - first, width), F32),
            jax.ShapeDtypeStruct((2, tall, width), F32),
            jax.ShapeDtypeStruct((4, heads, rows, width), BF16),
            jax.ShapeDtypeStruct(table.shape, F32),
        ),
        in_specs=[pl.BlockSpec(memory_space=pltpu.HBM)] * 5,
        out_specs=[pl.BlockSpec(memory_space=pltpu.VMEM)] * 5,
        scratch_shapes=[
            pltpu.VMEM((4, rows * heads, width), BF16),
            pltpu.VMEM((4, rows * heads, width), F32),
            pltpu.SemaphoreType.DMA((4, CHUNKS)),
            pltpu.SemaphoreType.DMA,
        ],
        compiler_params=pltpu.CompilerParams(vmem_limit_bytes=24 * 2**20),
        name="states",
    )(*[pltpu.with_memory_space_constraint(array, pltpu.HBM) for array in (*flat, table)])


def local_kernel(chosen, table_ref, per_head_ref, *refs):
    out_ref = refs[-1]
    rows = per_head_ref.shape[2]
    for head, sides in chosen:
        local_head(head, sides, rows, table_ref, per_head_ref.at[:, head], out_ref.at[:, head])


def local_head(head, sides, rows, table_ref, per_head_ref, out_ref):
    tiles = rows // TILE
    inner = (TILE // BLOCK).bit_length()
    weight = [weight_of(table_ref, head, level) for level in range(inner + tiles.bit_length() - 1)]
    row = lax.broadcasted_iota(jnp.int32, (TILE, TILE), 0)
    column = lax.broadcasted_iota(jnp.int32, (TILE, TILE), 1)
    apart = jnp.bitwise_xor(row // BLOCK, column // BLOCK)
    level_mask = jnp.where(apart == 0, weight[0], weight[1])
    for level in range(2, inner):
        level_mask = jnp.where(apart >= 1 << (level - 1), weight[level], level_mask)
    lower = jnp.where(row >= column, level_mask, 0.0)
    upper = jnp.where(row <= column, level_mask, 0.0)
    part = [[per_head_ref[which, pl.ds(tile * TILE, TILE), :] for tile in range(tiles)] for which in range(4)]
    queries, keys, values, out_grad = part

    def sums(states):
        table = {(0, tile): states[tile] for tile in range(tiles)}
        for bit in range(1, tiles.bit_length() - 1):
            for group in range(tiles >> bit):
                table[bit, group] = table[bit - 1, 2 * group] + table[bit - 1, 2 * group + 1]
        return table

    def gather(table, tile, side):
        total = None
        for bit in range(tiles.bit_length() - 1):
            if (tile >> bit) % 2 == side:
                term = weight[inner + bit] * table[bit, (tile >> bit) ^ 1]
                total = term if total is None else total + term
        return [] if total is None else split(total)

    turned = [[block.T for block in array] for array in part]
    q_t, k_t, v_t, g_t = turned
    if 0 in sides:
        key_sums = sums([dot_nn(k_t[tile], values[tile]) for tile in range(tiles)])
        key_sums_t = sums([dot_nn(v_t[tile], keys[tile]) for tile in range(tiles)])
    if 1 in sides:
        query_sums = sums([dot_nn(q_t[tile], out_grad[tile]) for tile in range(tiles)])
        query_sums_t = sums([dot_nn(g_t[tile], queries[tile]) for tile in range(tiles)])
    held = []
    for tile in range(tiles):
        q, k, v, g = (array[tile] for array in part)
        terms = []
        if 0 in sides:
            terms += [
                (0, dot_nn(q, k_t[tile]) * lower, v, q, gather(key_sums, tile, 1)),
                (1, dot_nn(g, v_t[tile]) * lower, k, g, gather(key_sums_t, tile, 1)),
            ]
        if 1 in sides:
            terms += [
                (2, dot_nn(v, g_t[tile]) * upper, q, v, gather(query_sums_t, tile, 0)),
                (3, dot_nn(k, q_t[tile]) * upper, g, k, gather(query_sums, tile, 0)),
            ]
        held.append(terms)
    for tile in range(tiles):
        for which, inside, other, mine, pieces in held[tile]:
            result = dot_nn(jnp.concatenate([*split(inside), *([mine, mine] if pieces else [])], 1), jnp.concatenate([other, other, *pieces], 0))
            out_ref[which, pl.ds(tile * TILE, TILE), :] = result


def local_part(chosen, flops, table, per_head, *earlier):
    vmem = pl.BlockSpec(memory_space=pltpu.VMEM)
    return pl.pallas_call(
        functools.partial(local_kernel, chosen),
        out_shape=jax.ShapeDtypeStruct(per_head.shape, F32),
        in_specs=[pl.BlockSpec(memory_space=pltpu.VMEM)] + [vmem] * (1 + len(earlier)),
        out_specs=vmem,
        input_output_aliases={2: 0} if earlier else {},
        compiler_params=pltpu.CompilerParams(vmem_limit_bytes=16 * 2**20),
        cost_estimate=pl.CostEstimate(flops=flops, bytes_accessed=flops // 1000, transcendentals=0),
        name="local",
    )(table, per_head, *earlier)


def far_states(table_ref, head, rows, near, pair, *groups):
    core, chip = lax.axis_index("rep"), lax.axis_index("seq")
    terms = [(core == 1, near), (chip % 2 == 1, pair)]
    terms += [((chip >> bit) % 2 == 1, group) for bit, group in enumerate(groups, 1)]
    keys_far = queries_far = 0.0
    for level, (later, piece) in enumerate(terms, (rows // BLOCK).bit_length()):
        weight = weight_of(table_ref, head, level)
        keys_far += jnp.where(later, weight, 0.0) * piece
        queries_far += jnp.where(later, 0.0, weight) * piece
    return [jnp.concatenate(split(state), 0) for state in (keys_far, keys_far.T, queries_far.T, queries_far)]


def far_heads(owner, table_ref, per_head_ref, local_ref, near, far_ref, wide_ref, finish=None, parts=1):
    heads, rows = per_head_ref.shape[1:3]
    half = heads // 2
    chosen = [owner * half + place for place in range(half)]
    width = far_ref.shape[2]
    spans = [slice(place * width, (place + 1) * width) for place in range(half)]
    states = [
        far_states(table_ref, head, rows, near(span), *[far_ref[bit, span] for bit in range(far_ref.shape[0])])
        for head, span in zip(chosen, spans)
    ]
    part = rows // parts
    for which, source in enumerate((0, 3, 2, 1)):
        for piece in range(parts):
            span = pl.ds(piece * part, part)
            for head, pieces in zip(chosen, states):
                mine = per_head_ref[source, head, span]
                result = local_ref[which, head, span] + dot_nn(jnp.concatenate([mine, mine], 1), pieces[which])
                wide_ref[which, pl.ds(piece * part * heads + head, part, stride=heads), :] = result
            if finish is not None:
                finish(which, pl.ds(piece * part * heads, part * heads))


def own_kernel(table_ref, per_head_ref, local_ref, received_a_ref, received_b_ref, far_ref, wide_ref):
    core = lax.axis_index("rep")
    far_heads(core, table_ref, per_head_ref, local_ref, lambda span: jnp.concatenate([received_a_ref[1 - core], received_b_ref[1 - core]], 0)[span],
              far_ref, wide_ref)


def last_kernel(table_ref, per_head_ref, local_ref, near_ref, far_ref, _, *refs):
    out_refs, (wide_ref, narrow, left) = refs[:4], refs[4:]
    copies = []

    def finish(which, span):
        narrow[which, span] = wide_ref[which, span].astype(BF16)
        copy = pltpu.make_async_copy(narrow.at[which, span], out_refs[which].at[span], left.at[len(copies)])
        copy.start()
        copies.append(copy)

    far_heads(1 - lax.axis_index("rep"), table_ref, per_head_ref, local_ref, lambda span: near_ref[span],
              far_ref, wide_ref, finish, PARTS)
    for copy in copies:
        copy.wait()


def own_part(table, per_head, *operands):
    _, heads, rows, width = per_head.shape
    vmem = pl.BlockSpec(memory_space=pltpu.VMEM)
    return pl.pallas_call(
        own_kernel,
        out_shape=jax.ShapeDtypeStruct((4, rows * heads, width), F32),
        in_specs=[pl.BlockSpec(memory_space=pltpu.VMEM)] + [vmem] * (1 + len(operands)),
        out_specs=vmem,
        compiler_params=pltpu.CompilerParams(vmem_limit_bytes=16 * 2**20),
        cost_estimate=pl.CostEstimate(flops=10**9, bytes_accessed=3 * 2**20, transcendentals=0),
        name="own",
    )(table, per_head, *operands)


def last_part(table, per_head, *operands):
    _, heads, rows, width = per_head.shape
    vmem = pl.BlockSpec(memory_space=pltpu.VMEM)
    wide = operands[-1]
    outs = pl.pallas_call(
        last_kernel,
        out_shape=[jax.ShapeDtypeStruct((rows * heads, width), BF16)] * 4 + [jax.ShapeDtypeStruct(wide.shape, F32)],
        in_specs=[pl.BlockSpec(memory_space=pltpu.VMEM)] + [vmem] * (1 + len(operands)),
        out_specs=[pl.BlockSpec(memory_space=pltpu.HBM)] * 4 + [vmem],
        scratch_shapes=[pltpu.VMEM((4, rows * heads, width), BF16), pltpu.SemaphoreType.DMA((4 * PARTS,))],
        input_output_aliases={1 + len(operands): 4},
        compiler_params=pltpu.CompilerParams(vmem_limit_bytes=16 * 2**20),
        name="last",
    )(table, per_head, *operands)
    return tuple(out.reshape(rows, heads, width) for out in outs[:4])


def load_kernel(keep_ref, received_a_ref, received_b_ref, pair_ref, rest_ref, near_ref):
    core, chip = lax.axis_index("rep"), lax.axis_index("seq")
    first = received_a_ref.shape[1]
    kind = chip % 2
    pair_ref[:first] = keep_ref[kind, :first] + received_a_ref[kind]
    pair_ref[first:] = keep_ref[kind, first:] + received_b_ref[kind]
    for bit in range(rest_ref.shape[0]):
        kind = (chip >> (bit + 1)) % 2
        rest_ref[bit] = keep_ref[kind, first:] + received_b_ref[kind]
    near_ref[...] = keep_ref[core]


def loads_of(bits, keep, *received):
    vmem = pl.BlockSpec(memory_space=pltpu.VMEM)
    tall, width = keep.shape[1:]
    shapes = ((tall, width), (bits - 1, received[1].shape[1], width), (tall, width))
    return pl.pallas_call(
        load_kernel,
        out_shape=[jax.ShapeDtypeStruct(shape, F32) for shape in shapes],
        in_specs=[vmem] * 3,
        out_specs=[vmem] * 3,
        compiler_params=pltpu.CompilerParams(vmem_limit_bytes=4 * 2**20),
        cost_estimate=pl.CostEstimate(flops=10**9, bytes_accessed=3 * 2**20, transcendentals=0),
        name="loads",
    )(keep, *received)


def per_device(queries, keys, values, out_grad, level_table):
    rows, heads, width = queries.shape
    half = heads // 2
    bits = lax.axis_size("seq").bit_length() - 1
    chip = lax.axis_index("seq")
    flat = [array.reshape(rows * heads, width) for array in (queries, keys, values, out_grad)]
    send_a, send_b, keep, per_head, table = states(flat, level_table.T)
    received_a, received_b = swap_cores(send_a), swap_cores(send_b)
    local_a = local_part([(0, (0,))], 10**9, table, per_head)
    received_a, per_head, local_a = lax.optimization_barrier((received_a, per_head, local_a))
    first_rows = received_a.shape[1]
    first = [
        jnp.where((chip >> bit) % 2 == 1, keep[1, :first_rows] + received_a[1], keep[0, :first_rows] + received_a[0])
        for bit in range(1, bits)
    ]
    first, keep, received_a = lax.optimization_barrier((first, keep, received_a))
    half_way = [
        sum(swap_chips(first[bit - 1], mask) for mask in range(1 << bit, 2 << bit, 2)) for bit in range(1, bits)
    ]
    pair_load, rest, near_load = loads_of(bits, keep, received_a, received_b)
    pair_load, rest, near_load, held = lax.optimization_barrier((pair_load, rest, near_load, per_head))
    group_b = [
        [swap_chips(rest[bit - 1], mask) for mask in range((2 << bit) - 1, (1 << bit) - 1, -1)] for bit in range(1, bits)
    ]
    pair = swap_chips(pair_load, 1)
    near = swap_cores(near_load)
    half_way = jnp.stack(half_way)
    half_way, held, local_a = lax.optimization_barrier((half_way, held, local_a))
    hop = swap_chips(half_way, 1)
    local_b = local_part([(0, (1,))] + [(head, (0, 1)) for head in range(1, heads)], 10**9, table, held, local_a)
    pair, hop, group_b, local_b = lax.optimization_barrier((pair, hop, group_b, local_b))
    group = jnp.concatenate([half_way + hop, jnp.stack([sum(pieces) for pieces in group_b])], 1)
    far = jnp.concatenate([pair[None], group])
    far_o = swap_cores(far)
    wide = own_part(table, per_head, local_b, received_a, received_b, far)
    return last_part(table, per_head, local_b, near, far_o, wide)


def solution(mesh):
    part = P(("groups", "seq", "rep"), "head", None)
    return jax.shard_map(
        per_device,
        mesh=mesh,
        in_specs=(part, part, part, part, P(None, "head")),
        out_specs=(part, part, part, part),
        check_vma=False,
    )
```
